256 devices in a mesh: dp: 2 (over core), seq: 32 (over y, z), head: 4 (over x).
Axes of the slice: x: 4, y: 4, z: 8, core: 2. Of those that a mesh axis runs over, the one named last changes fastest.
Arguments:
- inputs: bfloat16 [2, 8192, 8192], P('dp', 'seq', 'head'), may hold values from -6 to 6
- proj_b: bfloat16 [2, 8192, 128], P('dp', 'seq'), may hold values from -2 to 2
- proj_c: bfloat16 [2, 8192, 128], P('dp', 'seq'), may hold values from -2 to 2
- step_size: float32 [2, 128, 8192], P('dp', 'head', 'seq'), may hold values from 0.2 to 2
- decay_rate: float32 [128], P('head'), may hold values from 0 to 0.15
- skip_gain: float32 [128], P('head'), may hold values from 0.5 to 1.5
- doc_lengths: int32 [2, 32], P('dp'), may hold values from 1 to 4096, 8192 in all within a row
- grad_out: bfloat16 [2, 8192, 8192], P('dp', 'seq', 'head'), may hold values from -0.59765625 to 0.59765625
Outputs:
- grad_inputs: bfloat16 [2, 8192, 8192], P('dp', 'seq', 'head')
- grad_b: float32 [2, 8192, 128], P('dp', 'seq')
- grad_c: float32 [2, 8192, 128], P('dp', 'seq')
- grad_step: float32 [2, 128, 8192], P('dp', 'head', 'seq')
- grad_rate: float32 [128], P('head')
- grad_skip: float32 [128], P('head')
The draws below stay inside these ranges and needn't reach their ends.
Inputs may be any that keep to these rules, and one draw needn't show every extreme that they name: `doc_lengths`: each row holds the 32 lengths of one sequence's documents, summing to 8192; the longest is exactly 4096.
All inputs are finite; a program needn't handle non-finite values.
Results may differ from the reference program's by a relative error of at most 0.0015.
Values sent between devices are 32-bit elements; how exact they have to be, the bound alone decides.
A program may use at most 192 MiB of HBM per device.

```python
import math
import jax
import jax.numpy as jnp
import numpy as np
from jax import lax

H = 128
HEAD_DIM = 64
N = 128
SPAN = 256
TOK_DEV = 256
LENGTH = 8192
SEQS = 2
DOCS = 32


def draw_step_size(key, part):
    key = jax.random.fold_in(key, 7)
    pick_key, level_key, factor_key, lower_key = jax.random.split(key, 4)
    blocks = LENGTH // TOK_DEV
    lower_share = 0.34
    chosen = jax.random.uniform(pick_key, (SEQS, H, blocks, 1)) < lower_share
    level = jnp.exp(jax.random.uniform(level_key, (SEQS, H, blocks, 1), minval=math.log(0.25), maxval=math.log(0.8)))
    factor = jnp.exp(jax.random.uniform(factor_key, (SEQS, H, blocks, TOK_DEV), minval=math.log(0.8), maxval=math.log(2.5)))
    lower = jax.random.uniform(lower_key, (SEQS, H, blocks, TOK_DEV), minval=0.2, maxval=0.3)
    values = jnp.where(chosen, lower, level * factor)
    return jnp.clip(values, 0.2, 2.0).reshape(SEQS, H, LENGTH).astype(jnp.float32)


def draw_decay_rate(key, part):
    key = jax.random.fold_in(key, 11)
    pick_key, slow_key, quick_key = jax.random.split(key, 3)
    slow_share = 0.5
    chosen = jax.random.uniform(pick_key, (H,)) < slow_share
    slow_rate = jnp.exp(jax.random.uniform(slow_key, (H,), minval=math.log(0.1 / LENGTH), maxval=math.log(1.5 / LENGTH)))
    quick_rate = jnp.exp(jax.random.uniform(quick_key, (H,), minval=math.log(2.0 / LENGTH), maxval=math.log(0.15)))
    return jnp.where(chosen, slow_rate, quick_rate).astype(jnp.float32)


def block_scale(rng, shape, pieces, smallest, largest):
    def one(axis_at, blocks):
        draws = jax.random.uniform(jax.random.fold_in(jax.random.fold_in(rng, 6), axis_at), (blocks,), jnp.float32, smallest / len(pieces), largest / len(pieces))
        return jnp.repeat(jnp.exp(draws), shape[axis_at] // blocks).reshape((-1,) + (1,) * (len(shape) - axis_at - 1))

    gain = one(*pieces[0])
    for cut in pieces[1:]:
        gain = gain * one(*cut)
    return gain


def split_up(amount, total, bound, skew):
    weights = [(1 << 20) // math.isqrt(rank ** skew) + 1 for rank in range(2, amount + 1)]
    surplus, given = total - bound - (amount - 1), [1] * (amount - 1)
    while surplus > 0:
        free = [i for i in range(amount - 1) if given[i] < bound]
        mass, budget = sum([weights[i] for i in free]), surplus
        for i in free:
            extra = min(bound - given[i], max(1, budget * weights[i] // mass), surplus)
            given[i] = given[i] + extra
            surplus = surplus - extra
    return np.array([bound] + given)


def ragged(own_key, amount, total, bound, skew):
    if amount == 2:
        one = jax.random.randint(own_key, (), max(1, total - bound), min(bound, total - 1) + 1)
        return jnp.stack([one, total - one])
    sizes = jnp.asarray(split_up(amount, total, bound, skew), jnp.int32)
    pairs = (amount - 1) // 2
    source_of, receiver = sizes[1:1 + 2 * pairs:2], sizes[2:2 + 2 * pairs:2]
    slack = jnp.minimum(source_of - 1, bound - receiver)
    moved = jax.random.randint(jax.random.fold_in(own_key, 1), (pairs,), 0, 1 << 20) % (slack + 1)
    sizes = sizes.at[1:1 + 2 * pairs:2].set(source_of - moved).at[2:2 + 2 * pairs:2].set(receiver + moved)
    return sizes[jax.random.permutation(jax.random.fold_in(own_key, 2), amount)]


def scatter_about(rng, shape, deviation, reach, cuts=(), kind=jnp.bfloat16):
    result = deviation * jax.random.normal(rng, shape, jnp.float32)
    if cuts:
        result = result * block_scale(rng, shape, cuts, -0.22, 0.18)
    return jnp.clip(result, -reach, reach).astype(kind)


def setup_inputs(seed: int = 0) -> dict:
    keys = jax.random.split(jax.random.key(seed), 9)
    return {
        "inputs": scatter_about(keys[0], (SEQS, LENGTH, H * HEAD_DIM), 1.0, 6.0, ((0, 2), (1, 32), (2, 4))),
        "proj_b": scatter_about(keys[1], (SEQS, LENGTH, N), 0.3, 2.0, ((0, 2), (1, 32))),
        "proj_c": scatter_about(keys[2], (SEQS, LENGTH, N), 0.3, 2.0, ((0, 2), (1, 32))),
        "step_size": draw_step_size(jax.random.fold_in(keys[8], 71), 0),
        "decay_rate": draw_decay_rate(jax.random.fold_in(keys[8], 71), 0),
        "skip_gain": jnp.clip(0.5 + 1.0 * jax.random.uniform(keys[5], (H,), jnp.float32) ** block_scale(keys[5], (H,), ((0, 4),), -0.2, 0.2), 0.5, 1.5),
        "doc_lengths": jax.vmap(lambda own: ragged(own, DOCS, LENGTH, LENGTH // 2, 2))(jax.random.split(keys[6], SEQS)).reshape((SEQS, DOCS)).astype(jnp.int32),
        "grad_out": scatter_about(keys[7], (SEQS, LENGTH, H * HEAD_DIM), 0.1, 0.59765625, ((0, 2), (1, 32), (2, 4))),
    }


exact_mode = lax.Precision.HIGHEST

def span_step(state, inputs, skip_vec):
    x_span, b_span, c_span, log_span, doc_span, doc_before = inputs
    running = jnp.cumsum(log_span, axis=0).T
    width = doc_span.shape[0]
    order = jnp.arange(width)
    same_doc = (doc_span[:, None] == doc_span[None, :]) & (order[:, None] >= order[None, :])
    log_gap = running[:, :, None] - running[:, None, :]
    decay_mask = jnp.where(same_doc[None], jnp.exp(jnp.where(same_doc[None], log_gap, 0.0)), 0.0)
    scores = jnp.dot(c_span, b_span.T, precision=exact_mode)
    y_local = jnp.einsum('hts,shp->thp', decay_mask * scores[None], x_span, precision=exact_mode)
    entering = jnp.exp(running) * (doc_span == doc_before).astype(jnp.float32)[None, :]
    y_carry = jnp.einsum('tn,hpn->thp', c_span, state, precision=exact_mode) * entering.T[:, :, None]
    y_span = y_local + y_carry + skip_vec[None, :, None] * x_span
    final_doc = doc_span[-1]
    leaving = jnp.exp(running[:, -1:] - running) * (doc_span == final_doc).astype(jnp.float32)[None, :]
    carried = jnp.exp(running[:, -1]) * (final_doc == doc_before).astype(jnp.float32)
    added = jnp.einsum('hs,sn,shp->hpn', leaving, b_span, x_span, precision=exact_mode)
    new_state = carried[:, None, None] * state + added
    return (new_state, y_span)

def run_spans(x_tokens, b_tokens, c_tokens, log_decay, doc_ids, doc_before, state, skip_vec, span):
    count = x_tokens.shape[0] // span
    befores = jnp.concatenate([doc_before, doc_ids[span - 1::span][:-1]])

    def split(array):
        return array.reshape((count, span) + array.shape[1:])

    def advance(carry, inputs):
        return span_step(carry, inputs, skip_vec)
    final_state, outputs = lax.scan(advance, state, (split(x_tokens), split(b_tokens), split(c_tokens), split(log_decay), split(doc_ids), befores))
    return (outputs.reshape(x_tokens.shape), final_state)

def document_ids(lengths, positions):
    starts = jnp.cumsum(lengths) - lengths
    return (lax.optimization_barrier(jnp.sum((positions[:, None] >= starts[None, :]).astype(jnp.int32), axis=1)) - 1).astype(jnp.int32)

def group_grads(x_group, b_float, c_float, step_group, rate_group, skip_group, dy_group, doc_ids, doc_before):

    def forward(x_in, b_in, c_in, step_in, rate_in, skip_in):
        log_decay = -(step_in * rate_in[:, None]).T
        state = jnp.zeros((x_in.shape[1], x_in.shape[2], b_in.shape[1]), jnp.float32)
        y_out, final_state = run_spans(x_in, b_in, c_in, log_decay, doc_ids, doc_before, state, skip_in, SPAN)
        return y_out
    unused, pullback = jax.vjp(forward, x_group.astype(jnp.float32), b_float, c_float, step_group, rate_group, skip_group)
    return pullback(dy_group.astype(jnp.float32))

def reference(inputs, proj_b, proj_c, step_size, decay_rate, skip_gain, doc_lengths, grad_out):
    group = 8
    groups = H // group
    grad_x_list, grad_b_list, grad_c_list, grad_step_list = ([], [], [], [])
    rate_total = jnp.zeros((H,), jnp.float32)
    skip_total = jnp.zeros((H,), jnp.float32)
    positions = jnp.arange(LENGTH, dtype=jnp.int32)
    for sequence in range(SEQS):
        doc_ids = document_ids(doc_lengths[sequence], positions)
        doc_before = jnp.full((1,), -1, jnp.int32)
        x_stack = inputs[sequence].reshape(LENGTH, groups, group, HEAD_DIM).transpose(1, 0, 2, 3)
        dy_stack = grad_out[sequence].reshape(LENGTH, groups, group, HEAD_DIM).transpose(1, 0, 2, 3)
        step_stack = step_size[sequence].reshape(groups, group, LENGTH)
        b_float = proj_b[sequence].astype(jnp.float32)
        c_float = proj_c[sequence].astype(jnp.float32)

        def one_group(items):
            x_group, dy_group, step_group, rate_group, skip_group = items
            return group_grads(x_group, b_float, c_float, step_group, rate_group, skip_group, dy_group, doc_ids, doc_before)
        grad_x, grad_bs, grad_cs, grad_steps, grad_rates, grad_skips = lax.map(one_group, (x_stack, dy_stack, step_stack, decay_rate.reshape(groups, group), skip_gain.reshape(groups, group)))
        grad_x_list.append(grad_x.transpose(1, 0, 2, 3).reshape(LENGTH, H * HEAD_DIM).astype(jnp.bfloat16))
        grad_b_list.append(lax.optimization_barrier(jnp.sum(grad_bs, axis=0)))
        grad_c_list.append(lax.optimization_barrier(jnp.sum(grad_cs, axis=0)))
        grad_step_list.append(grad_steps.reshape(H, LENGTH))
        rate_total = rate_total + grad_rates.reshape(H)
        skip_total = skip_total + grad_skips.reshape(H)
    return (jnp.stack(grad_x_list), jnp.stack(grad_b_list), jnp.stack(grad_c_list), jnp.stack(grad_step_list), rate_total, skip_total)
```

```python
import jax
import jax.numpy as jnp
from jax import lax
from jax.experimental import pallas as pl
from jax.experimental.pallas import tpu as pltpu
from jax.sharding import PartitionSpec as P

F32 = jnp.float32
BF16 = jnp.bfloat16
MESH = pl.DeviceIdType.MESH

ROWS = 4
RING = 8
SEQ = ROWS * RING
HEADS_AX = 4
TOK = 256
HEADS = 32
HEAD_DIM = 64
STATE = 128
FEAT = HEADS * HEAD_DIM
WIDE = 256
GROUPS = FEAT // WIDE
SLICES = 4 * GROUPS
HALF = STATE // 2
MSG = 2 * HALF + 8
LAG = 3


def nn(a, b):
    return lax.dot_general(a, b, (((1,), (0,)), ((), ())), preferred_element_type=F32)


def nt(a, b):
    return lax.dot_general(a, b, (((1,), (1,)), ((), ())), preferred_element_type=F32)


def split2(value):
    high = value.astype(BF16)
    return high, (value - high.astype(F32)).astype(BF16)


def split3(value):
    high = value.astype(BF16)
    rest = value - high.astype(F32)
    middle = rest.astype(BF16)
    return high, middle, (rest - middle.astype(F32)).astype(BF16)


def iota(shape, dim):
    return lax.broadcasted_iota(jnp.int32, shape, dim)


def kernel(
    x_ref,
    dy_ref,
    b_ref,
    c_ref,
    step_ref,
    rate_ref,
    skip_ref,
    len_ref,
    gx_ref,
    gb_ref,
    gc_ref,
    gs_ref,
    gr_ref,
    gk_ref,
    xh_ref,
    xl_ref,
    dyh_ref,
    dyl_ref,
    em_ref,
    dx_ref,
    yl_ref,
    ob_ref,
    rt_ref,
    sm_ref,
    smt_ref,
    ds_ref,
    cb_ref,
    cbt_ref,
    g_ref,
    th_ref,
    skx_ref,
    sk_ref,
    rc_ref,
    l_ref,
    ld_ref,
    recv_p,
    recv_m,
    send_p,
    send_m,
    cin_s,
    cin_d,
    ysend_s,
    ysend_d,
    sp_ref,
    dp_ref,
    acc_ref,
    part_ref,
    rs_ref,
    sum_ref,
    full_ref,
    vec_ref,
    vdp_ref,
    vec2_ref,
    vz_ref,
    vec3_ref,
    vy_ref,
    p_send,
    p_recv,
    m_send,
    m_recv,
    s_send,
    s_recv,
    d_send,
    d_recv,
    rs_send,
    rs_recv,
    ag_send,
    ag_recv,
    v_send,
    v_recv,
):
    core = lax.axis_index("dp")
    k = lax.axis_index("seq")
    head = lax.axis_index("head")
    y = k // RING
    z = lax.rem(k, RING)
    right = lax.rem(k + 1, SEQ)
    left = lax.rem(k + SEQ - 1, SEQ)
    up = lax.rem(k + RING, SEQ)
    down = lax.rem(k + SEQ - RING, SEQ)

    peers = [{"seq": right}, {"seq": left}, {"dp": 1 - core}]
    peers += [{"seq": y * RING + lax.rem(z + d, RING)} for d in range(1, RING)]
    peers += [{"seq": lax.rem(y + d, ROWS) * RING + z} for d in range(1, ROWS)]
    peers += [{"head": lax.rem(head + d, HEADS_AX)} for d in range(1, HEADS_AX)]
    barrier = pltpu.get_barrier_semaphore()
    for peer in peers:
        pl.semaphore_signal(barrier, inc=1, device_id=peer, device_id_type=MESH)

    lens = len_ref[...].astype(F32)
    docs = lens.shape[1]
    sub, lane = iota((docs, docs), 0), iota((docs, docs), 1)
    lens_col = jnp.sum(jnp.where(sub == lane, lens, 0.0), axis=1, keepdims=True)
    ends_row = jnp.sum(jnp.where(sub <= lane, lens_col, 0.0), axis=0, keepdims=True)
    ends_col = jnp.sum(jnp.where(lane <= sub, lens, 0.0), axis=1, keepdims=True)
    anchor = k * TOK
    pos_c = (anchor + iota((TOK, docs), 0)).astype(F32)
    pos_r = (anchor + iota((docs, TOK), 1)).astype(F32)
    one_r = (anchor + iota((1, docs), 0)).astype(F32)
    doc_c = jnp.sum(jnp.where(ends_row <= pos_c, 1.0, 0.0), axis=1, keepdims=True)
    doc_r = jnp.sum(jnp.where(ends_col <= pos_r, 1.0, 0.0), axis=0, keepdims=True)
    before = jnp.sum(jnp.where(ends_row <= one_r - 1.0, 1.0, 0.0), axis=1, keepdims=True)
    before = jnp.where(one_r[:, :1] < 0.5, -1.0, before)
    last = jnp.sum(jnp.where(ends_row <= one_r + (TOK - 1.0), 1.0, 0.0), axis=1, keepdims=True)
    enter = jnp.where(doc_c == before, 1.0, 0.0)
    leave = jnp.where(doc_c == last, 1.0, 0.0)
    same_end = jnp.where(last == before, 1.0, 0.0)

    bq, cq = b_ref[...], c_ref[...]
    rows, cols = iota((TOK, TOK), 0), iota((TOK, TOK), 1)
    same = doc_c == doc_r
    lower = same & (rows >= cols)
    sm_ref[0], sm_ref[1] = split2(jnp.where(lower, nt(cq, bq), 0.0))
    smt_ref[0], smt_ref[1] = split2(jnp.where(same & (rows <= cols), nt(bq, cq), 0.0))
    cm, bm = cq.astype(F32) * enter, bq.astype(F32) * leave
    cb_ref[0], cb_ref[1] = cm.astype(BF16), bm.astype(BF16)
    cbt_ref[0], cbt_ref[1] = cm.T.astype(BF16), bm.T.astype(BF16)

    hsub, hlane = iota((HEADS, HEADS), 0), iota((HEADS, HEADS), 1)
    rate_col = jnp.sum(jnp.where(hsub == hlane, rate_ref[...], 0.0), axis=1, keepdims=True)
    skip_col = jnp.sum(jnp.where(hsub == hlane, skip_ref[...], 0.0), axis=1, keepdims=True)
    step = step_ref[...]
    tri = jnp.where(rows >= cols, 1.0, 0.0).astype(BF16)
    owner = jnp.where(iota((HEADS, FEAT), 1) // HEAD_DIM == iota((HEADS, FEAT), 0), 1.0, 0.0)
    ob_ref[...] = owner.astype(BF16)
    skx_ref[...] = jnp.sum(owner * skip_col, axis=0, keepdims=True)
    running = sum(nt(tri, part) for part in split3(-(step * rate_col)))
    rt_ref[0], rt_ref[1], rt_ref[2] = split3(running)

    def prepare(i, _):
        at = pl.ds(pl.multiple_of(i * WIDE, WIDE), WIDE)
        ob = ob_ref[:, at]
        rx = nn(rt_ref[0], ob) + nn(rt_ref[1], ob) + nn(rt_ref[2], ob)
        end = rx[TOK - 1 : TOK, :]
        mid = 0.5 * end
        em = jnp.exp(mid - rx)
        em_ref[:, at] = em
        x_f, dy_f = x_ref[:, at].astype(F32), dy_ref[:, at].astype(F32)
        sk_ref[:, at] = jnp.broadcast_to(jnp.sum(x_f * dy_f, axis=0, keepdims=True), (8, WIDE))
        xh, xl = split2(em * x_f)
        dyh, dyl = split2(jnp.exp(rx - mid) * dy_f)
        xh_ref[:, at], xl_ref[:, at], dyh_ref[:, at], dyl_ref[:, at] = xh, xl, dyh, dyl
        g = jnp.exp(mid)
        th = jnp.exp(end) * same_end
        local = g * (nn(cbt_ref[1], xh) + nn(cbt_ref[1], xl))
        local_d = g * (nn(cbt_ref[0], dyh) + nn(cbt_ref[0], dyl))
        for q in range(2):
            cut = slice(q * 128, q * 128 + 128)
            g_ref[2 * i + q] = jnp.broadcast_to(g[:, cut], (8, 128))
            th_ref[2 * i + q] = jnp.broadcast_to(th[:, cut], (8, 128))
            for half in range(2):
                some = slice(half * HALF, half * HALF + HALF)
                l_ref[4 * i + 2 * q + half] = local[some, cut]
                ld_ref[4 * i + 2 * q + half] = local_d[some, cut]
        return 0

    lax.fori_loop(0, GROUPS, prepare, 0)
    rc_ref[...] = jnp.zeros_like(rc_ref)
    ds_ref[...] = jnp.zeros_like(ds_ref)
    pl.semaphore_wait(barrier, len(peers))

    def remote(src, dst, send, recv, device):
        return pltpu.make_async_remote_copy(
            src_ref=src,
            dst_ref=dst,
            send_sem=send,
            recv_sem=recv,
            device_id=device,
            device_id_type=MESH,
        )

    def copy_p(s):
        return remote(send_p.at[s], recv_p.at[s], p_send.at[s], p_recv.at[s], {"seq": right})

    def copy_m(s):
        return remote(send_m.at[s], recv_m.at[s], m_send.at[s], m_recv.at[s], {"seq": left})

    def copy_s(s):
        return remote(ysend_s.at[s], cin_s.at[s], s_send.at[s], s_recv.at[s], {"seq": up})

    def copy_d(s):
        return remote(ysend_d.at[s], cin_d.at[s], d_send.at[s], d_recv.at[s], {"seq": down})

    def chain(s, first, final, edge, copy, recv, send, mine, other):
        @pl.when(first)
        def _():
            recv[s, : 2 * HALF] = jnp.zeros((2 * HALF, 128), F32)
            recv[s, 2 * HALF :] = jnp.ones((8, 128), F32)

        @pl.when(jnp.logical_not(first))
        def _():
            copy(s).wait_recv()

            @pl.when(edge)
            def _():
                recv[s, :HALF] = jnp.zeros((HALF, 128), F32)
                recv[s, 2 * HALF :] = jnp.zeros((8, 128), F32)

        @pl.when(jnp.logical_not(final))
        def _():
            weight = recv[s, 2 * HALF :]
            send[s, HALF : 2 * HALF] = recv[s, HALF : 2 * HALF] + weight[:1] * other[s]
            send[s, 2 * HALF :] = weight * th_ref[s // 2]

        send[s, :HALF] = th_ref[s // 2, 0:1] * recv[s, :HALF] + mine[s]

        @pl.when(jnp.logical_not(final))
        def _():
            copy(s).start()

    def total_s(s):
        return recv_m[s, 2 * HALF : 2 * HALF + 1] * send_p[s, :HALF] + recv_m[s, HALF : 2 * HALF]

    def total_d(s):
        return recv_p[s, 2 * HALF : 2 * HALF + 1] * send_m[s, :HALF] + recv_p[s, HALF : 2 * HALF]

    def finish(s, has_recv, has_send, total, copy, cin, ysend, own, own_weight, dest):
        weight_p = recv_p[s, 2 * HALF : 2 * HALF + 1]
        weight_m = recv_m[s, 2 * HALF : 2 * HALF + 1]

        @pl.when(has_recv)
        def _():
            copy(s).wait_recv()

        @pl.when(jnp.logical_not(has_recv))
        def _():
            cin[s] = jnp.zeros((HALF, 128), F32)

        @pl.when(has_send)
        def _():
            through = weight_p * weight_m * th_ref[s // 2, 0:1]
            ysend[s] = total(s) + through * cin[s]
            copy(s).start()

        weight = weight_p if own_weight else weight_m
        state = own[s, :HALF] + weight * cin[s]
        cin[s] = state
        dest[0, s], dest[1, s] = split2(state * g_ref[s // 2, 0:1])

    def at_slot(slot, which):
        hop = slot // 4
        o = hop if which == 0 else RING - 1 - hop
        group = lax.rem(z - o + RING, RING)
        return group, 4 * group + lax.rem(slot, 4)

    def ywork(tau):
        fresh = (tau >= 16) & (tau < 32)
        for which in range(2):
            group, s = at_slot(jnp.clip(tau, 0, 31), which)

            @pl.when(fresh & (y == ROWS - 1) & (group > 0) & (z >= group))
            def _():
                ysend_s[s] = total_s(s)
                copy_s(s).start()

            @pl.when(fresh & (y == 0) & (z < group))
            def _():
                ysend_d[s] = total_d(s)
                copy_d(s).start()

        for wrap in range(2):
            for which in range(2):
                slot = tau - LAG * (y + wrap)
                group, s = at_slot(jnp.clip(slot, 0, 31), which)
                wraps = (group > 0) & (z >= group)
                mine = wraps if wrap else jnp.logical_not(wraps)

                @pl.when((slot >= 16) & (slot < 32) & mine)
                def _():
                    finish(
                        s,
                        y + wrap > 0,
                        y < ROWS - 1,
                        total_s,
                        copy_s,
                        cin_s,
                        ysend_s,
                        recv_p,
                        True,
                        sp_ref,
                    )

                slot_d = tau - LAG * (ROWS - 1 - y + wrap)
                group_d, s_d = at_slot(jnp.clip(slot_d, 0, 31), which)
                mine_d = z < group_d if wrap else z >= group_d

                @pl.when((slot_d >= 16) & (slot_d < 32) & mine_d)
                def _():
                    finish(
                        s_d,
                        ROWS - 1 - y + wrap > 0,
                        y > 0,
                        total_d,
                        copy_d,
                        cin_d,
                        ysend_d,
                        recv_m,
                        False,
                        dp_ref,
                    )

    def own_heads(i):
        shape = (WIDE, 128)
        hit = iota(shape, 0) // HEAD_DIM + 4 * i == iota(shape, 1)
        return jnp.where(hit, 1.0, 0.0).astype(BF16)

    def add_products(i, at, y_part, dx_part, extra):
        dyp = dyh_ref[:, at].astype(F32) + dyl_ref[:, at].astype(F32)
        xp = xh_ref[:, at].astype(F32) + xl_ref[:, at].astype(F32)
        prod = dyp * y_part - xp * dx_part
        if extra is not None:
            prod = prod + jnp.where(iota((TOK, WIDE), 0) == TOK - 1, extra, 0.0)
        heads = own_heads(i)
        rc_ref[...] += sum(nn(part, heads) for part in split3(prod))

    def local_work(tau):
        i = tau // 4
        at = pl.ds(pl.multiple_of(i * WIDE, WIDE), WIDE)
        turn = lax.rem(tau, 4)

        @pl.when(turn == 0)
        def _():
            yl_ref[...] = (
                nn(sm_ref[0], xh_ref[:, at])
                + nn(sm_ref[0], xl_ref[:, at])
                + nn(sm_ref[1], xh_ref[:, at])
            )

        @pl.when(turn == 1)
        def _():
            dx_ref[:, at] = (
                nn(smt_ref[0], dyh_ref[:, at])
                + nn(smt_ref[0], dyl_ref[:, at])
                + nn(smt_ref[1], dyh_ref[:, at])
            )

        @pl.when(turn == 2)
        def _():
            add_products(i, at, yl_ref[...], dx_ref[:, at], None)

        @pl.when(turn == 3)
        def _():
            ds_ref[...] += (
                nt(dyh_ref[:, at], xh_ref[:, at])
                + nt(dyh_ref[:, at], xl_ref[:, at])
                + nt(dyl_ref[:, at], xh_ref[:, at])
            )

    def slot_body(tau, _):
        @pl.when(tau < 32)
        def _():
            hop = tau // 4
            group, s = at_slot(tau, 0)
            chain(s, hop == 0, hop == RING - 1, k == 0, copy_p, recv_p, send_p, l_ref, ld_ref)
            group, s = at_slot(tau, 1)
            chain(s, hop == 0, hop == RING - 1, k == SEQ - 1, copy_m, recv_m, send_m, ld_ref, l_ref)
            local_work(tau)

        @pl.when(tau >= 16)
        def _():
            ywork(tau)

        return 0

    lax.fori_loop(0, 32 + LAG * ROWS, slot_body, 0)

    def states(ref, part, i):
        a, b, c, d = (ref[part, 4 * i + n] for n in range(4))
        top = jnp.concatenate([a, c], axis=1)
        return jnp.concatenate([top, jnp.concatenate([b, d], axis=1)], axis=0)

    acc_ref[...] = jnp.zeros_like(acc_ref)

    def grads_bc(i, _):
        at = pl.ds(pl.multiple_of(i * WIDE, WIDE), WIDE)
        sh, sl = states(sp_ref, 0, i), states(sp_ref, 1, i)
        dh, dl = states(dp_ref, 0, i), states(dp_ref, 1, i)
        xh, xl, dyh, dyl = xh_ref[:, at], xl_ref[:, at], dyh_ref[:, at], dyl_ref[:, at]
        acc_ref[:, :STATE] += nt(xh, dh) + nt(xl, dh) + nt(xh, dl)
        acc_ref[:, STATE:] += nt(dyh, sh) + nt(dyl, sh) + nt(dyh, sl)
        return 0

    lax.fori_loop(0, GROUPS, grads_bc, 0)
    d_scores = jnp.where(lower, ds_ref[...], 0.0)
    sh, sl = split2(d_scores)
    th, tl = split2(d_scores.T)
    part_ref[:, :STATE] = leave * acc_ref[:, :STATE] + nn(th, cq) + nn(tl, cq)
    part_ref[:, STATE:] = enter * acc_ref[:, STATE:] + nn(sh, bq) + nn(sl, bq)
    quarter = TOK // HEADS_AX

    def copy_rs(d):
        target = lax.rem(head + d, HEADS_AX)
        rows_of = pl.ds(pl.multiple_of(target * quarter, quarter), quarter)
        return remote(
            part_ref.at[rows_of], rs_ref.at[d], rs_send.at[d], rs_recv.at[d], {"head": target}
        )

    def copy_ag(d):
        target = lax.rem(head + d, HEADS_AX)
        return remote(
            sum_ref, full_ref.at[head], ag_send.at[d], ag_recv.at[d], {"head": target}
        )

    def wait_ag(d):
        source = lax.rem(head + HEADS_AX - d, HEADS_AX)
        target = lax.rem(head + d, HEADS_AX)
        return remote(
            sum_ref, full_ref.at[source], ag_send.at[d], ag_recv.at[d], {"head": target}
        )

    for d in range(1, HEADS_AX):
        copy_rs(d).start()

    def grads_x(i):
        at = pl.ds(pl.multiple_of(i * WIDE, WIDE), WIDE)
        y_part = nn(cb_ref[0], states(sp_ref, 0, i)) + nn(cb_ref[0], states(sp_ref, 1, i))
        dx_part = nn(cb_ref[1], states(dp_ref, 0, i)) + nn(cb_ref[1], states(dp_ref, 1, i))
        ends = []
        for q in range(2):
            total = 0.0
            for half in range(2):
                s = 4 * i + 2 * q + half
                out = th_ref[2 * i + q, 0:1] * cin_s[s] + l_ref[s]
                total = total + jnp.sum(out * cin_d[s], axis=0, keepdims=True)
            ends.append(total)
        add_products(i, at, y_part, dx_part, jnp.concatenate(ends, axis=1))
        whole = em_ref[:, at] * (dx_ref[:, at] + dx_part)
        whole = whole + skx_ref[:, at] * dy_ref[:, at].astype(F32)
        gx_ref[:, at] = whole.astype(BF16)

    def grads_x_step(i, _):
        grads_x(i)
        return 0

    lax.fori_loop(0, GROUPS, grads_x_step, 0)

    mine_rows = pl.ds(pl.multiple_of(head * quarter, quarter), quarter)
    for d in range(1, HEADS_AX):
        copy_rs(d).wait()
    sum_ref[...] = part_ref[mine_rows] + rs_ref[1] + rs_ref[2] + rs_ref[3]
    full_ref[head] = sum_ref[...]
    for d in range(1, HEADS_AX):
        copy_ag(d).start()

    dl = sum(nn(part[:HEADS], tri) for part in split3(rc_ref[...].T))
    gs_ref[...] = -(rate_col * dl)
    rate_part = -jnp.sum(step * dl, axis=1, keepdims=True)
    skip_part = sum(nt(ob_ref[...], part) for part in split3(sk_ref[...]))[:, :1]
    diag = iota((HEADS, 128), 0) == iota((HEADS, 128), 1)
    rate_row = jnp.sum(jnp.where(diag, rate_part, 0.0), axis=0, keepdims=True)
    skip_row = jnp.sum(jnp.where(diag, skip_part, 0.0), axis=0, keepdims=True)
    first = iota((8, 128), 0)
    vec_ref[...] = jnp.where(first == 0, rate_row, jnp.where(first == 1, skip_row, 0.0))

    swap = remote(vec_ref, vdp_ref, v_send.at[0], v_recv.at[0], {"dp": 1 - core})
    swap.start()
    swap.wait()
    vec2_ref[...] = vec_ref[...] + vdp_ref[...]
    vz_ref[z] = vec2_ref[...]

    def copy_z(d, slot):
        target = y * RING + lax.rem(z + d, RING)
        return remote(vec2_ref, vz_ref.at[slot], v_send.at[d], v_recv.at[d], {"seq": target})

    for d in range(1, RING):
        copy_z(d, z).start()
    for d in range(1, RING):
        copy_z(d, lax.rem(z + RING - d, RING)).wait()
    vec3_ref[...] = sum(vz_ref[n] for n in range(RING))
    vy_ref[y] = vec3_ref[...]

    def copy_y(d, slot):
        target = lax.rem(y + d, ROWS) * RING + z
        n = RING + d
        return remote(vec3_ref, vy_ref.at[slot], v_send.at[n], v_recv.at[n], {"seq": target})

    for d in range(1, ROWS):
        copy_y(d, y).start()
    for d in range(1, ROWS):
        copy_y(d, lax.rem(y + ROWS - d, ROWS)).wait()
    whole_vec = sum(vy_ref[n] for n in range(ROWS))
    gr_ref[...] = whole_vec[0:1, :HEADS]
    gk_ref[...] = whole_vec[1:2, :HEADS]

    for d in range(1, HEADS_AX):
        wait_ag(d).wait()
    for n in range(HEADS_AX):
        gb_ref[n * quarter : (n + 1) * quarter] = full_ref[n, :, :STATE]
        gc_ref[n * quarter : (n + 1) * quarter] = full_ref[n, :, STATE:]

    def drain(s, _):
        group = s // 4
        o = lax.rem(z - group + RING, RING)

        @pl.when(o < RING - 1)
        def _():
            copy_p(s).wait_send()

        @pl.when(o > 0)
        def _():
            copy_m(s).wait_send()

        @pl.when((y < ROWS - 1) | ((group > 0) & (z >= group)))
        def _():
            copy_s(s).wait_send()

        @pl.when((y > 0) | (z < group))
        def _():
            copy_d(s).wait_send()

        return 0

    lax.fori_loop(0, SLICES, drain, 0)


def on_device(inputs, proj_b, proj_c, step_size, decay_rate, skip_gain, doc_lengths, grad_out):
    vmem = pl.BlockSpec(memory_space=pltpu.VMEM)
    state = pltpu.VMEM((SLICES, HALF, 128), F32)
    message = pltpu.VMEM((SLICES, MSG, 128), F32)
    pair = pltpu.VMEM((2, SLICES, HALF, 128), BF16)
    sems = pltpu.SemaphoreType.DMA((SLICES,))
    tile = pltpu.VMEM((8, 128), F32)
    quarter = TOK // HEADS_AX
    scratch = [
        pltpu.VMEM((TOK, FEAT), BF16),
        pltpu.VMEM((TOK, FEAT), BF16),
        pltpu.VMEM((TOK, FEAT), BF16),
        pltpu.VMEM((TOK, FEAT), BF16),
        pltpu.VMEM((TOK, FEAT), F32),
        pltpu.VMEM((TOK, FEAT), F32),
        pltpu.VMEM((TOK, WIDE), F32),
        pltpu.VMEM((HEADS, FEAT), BF16),
        pltpu.VMEM((3, TOK, HEADS), BF16),
        pltpu.VMEM((2, TOK, TOK), BF16),
        pltpu.VMEM((2, TOK, TOK), BF16),
        pltpu.VMEM((TOK, TOK), F32),
        pltpu.VMEM((2, TOK, STATE), BF16),
        pltpu.VMEM((2, STATE, TOK), BF16),
        pltpu.VMEM((FEAT // 128, 8, 128), F32),
        pltpu.VMEM((FEAT // 128, 8, 128), F32),
        pltpu.VMEM((1, FEAT), F32),
        pltpu.VMEM((8, FEAT), F32),
        pltpu.VMEM((TOK, 128), F32),
        state,
        state,
        message,
        message,
        message,
        message,
        state,
        state,
        state,
        state,
        pair,
        pair,
        pltpu.VMEM((TOK, 2 * STATE), F32),
        pltpu.VMEM((TOK, 2 * STATE), F32),
        pltpu.VMEM((HEADS_AX, quarter, 2 * STATE), F32),
        pltpu.VMEM((quarter, 2 * STATE), F32),
        pltpu.VMEM((HEADS_AX, quarter, 2 * STATE), F32),
        tile,
        tile,
        tile,
        pltpu.VMEM((RING, 8, 128), F32),
        tile,
        pltpu.VMEM((ROWS, 8, 128), F32),
        sems,
        sems,
        sems,
        sems,
        sems,
        sems,
        sems,
        sems,
        pltpu.SemaphoreType.DMA((HEADS_AX,)),
        pltpu.SemaphoreType.DMA((HEADS_AX,)),
        pltpu.SemaphoreType.DMA((HEADS_AX,)),
        pltpu.SemaphoreType.DMA((HEADS_AX,)),
        pltpu.SemaphoreType.DMA((RING + ROWS,)),
        pltpu.SemaphoreType.DMA((RING + ROWS,)),
    ]
    grad_x, grad_b, grad_c, grad_step, grad_rate, grad_skip = pl.pallas_call(
        kernel,
        out_shape=(
            jax.ShapeDtypeStruct((TOK, FEAT), BF16),
            jax.ShapeDtypeStruct((TOK, STATE), F32),
            jax.ShapeDtypeStruct((TOK, STATE), F32),
            jax.ShapeDtypeStruct((HEADS, TOK), F32),
            jax.ShapeDtypeStruct((1, HEADS), F32),
            jax.ShapeDtypeStruct((1, HEADS), F32),
        ),
        in_specs=[vmem] * 8,
        out_specs=(vmem,) * 6,
        scratch_shapes=scratch,
        compiler_params=pltpu.CompilerParams(
            collective_id=0, has_side_effects=True, vmem_limit_bytes=56 << 20
        ),
    )(
        inputs[0],
        grad_out[0],
        proj_b[0],
        proj_c[0],
        step_size[0],
        decay_rate[None],
        skip_gain[None],
        doc_lengths,
    )
    return (
        grad_x[None],
        grad_b[None],
        grad_c[None],
        grad_step[None],
        grad_rate[0],
        grad_skip[0],
    )


def solution(mesh):
    in_specs = (
        P("dp", "seq", "head"),
        P("dp", "seq", None),
        P("dp", "seq", None),
        P("dp", "head", "seq"),
        P("head"),
        P("head"),
        P("dp", None),
        P("dp", "seq", "head"),
    )
    out_specs = (
        P("dp", "seq", "head"),
        P("dp", "seq", None),
        P("dp", "seq", None),
        P("dp", "head", "seq"),
        P("head"),
        P("head"),
    )
    return jax.shard_map(
        on_device, mesh=mesh, in_specs=in_specs, out_specs=out_specs, check_vma=False
    )
```

```python
import jax
import jax.numpy as jnp
from jax import lax
from jax.experimental import pallas as pl
from jax.experimental.pallas import tpu as pltpu
from jax.sharding import PartitionSpec as P

F32 = jnp.float32
BF16 = jnp.bfloat16
MESH = pl.DeviceIdType.MESH

ROWS = 4
RING = 8
SEQ = ROWS * RING
HEADS_AX = 4
TOK = 256
HEADS = 32
HEAD_DIM = 64
STATE = 128
FEAT = HEADS * HEAD_DIM
WIDE = 256
GROUPS = FEAT // WIDE
PIECES = 2
PER = 2 * PIECES
SLICES = PER * GROUPS
HALF = STATE // PIECES
LATE = SLICES // 2
HOP = 3 * PIECES // 2
LAG = 3 * PIECES // 2
DELAY = PER + 2
SLOTS = HOP * (RING - 1) + SLICES
ORDER = (0, 1, 4, 2, 5, 3, 6, 7)


def nn(a, b):
    return lax.dot_general(a, b, (((1,), (0,)), ((), ())), preferred_element_type=F32)


def nt(a, b):
    return lax.dot_general(a, b, (((1,), (1,)), ((), ())), preferred_element_type=F32)


def split2(value):
    high = value.astype(BF16)
    return high, (value - high.astype(F32)).astype(BF16)


def split3(value):
    high = value.astype(BF16)
    rest = value - high.astype(F32)
    middle = rest.astype(BF16)
    return high, middle, (rest - middle.astype(F32)).astype(BF16)


def over(n, size):
    return lax.shift_right_arithmetic(n, jnp.int32(size.bit_length() - 1))


def left_over(n, size):
    return lax.bitwise_and(n, jnp.int32(size - 1))


def iota(shape, dim):
    return lax.broadcasted_iota(jnp.int32, shape, dim)


def kernel(
    x_ref,
    dy_ref,
    b_ref,
    c_ref,
    step_ref,
    rate_ref,
    skip_ref,
    len_ref,
    gx_ref,
    gb_ref,
    gc_ref,
    gs_ref,
    gr_ref,
    gk_ref,
    xh_ref,
    xl_ref,
    dyh_ref,
    dyl_ref,
    em_ref,
    dx_ref,
    yl_ref,
    ob_ref,
    rt_ref,
    sm_ref,
    smt_ref,
    ds_ref,
    cb_ref,
    cbt_ref,
    g_ref,
    th_ref,
    w_ref,
    thz_ref,
    mask_ref,
    skx_ref,
    sk_ref,
    rc_ref,
    l_ref,
    ld_ref,
    recv_p,
    recv_m,
    send_p,
    send_m,
    cin_s,
    cin_d,
    ysend_s,
    ysend_d,
    sp_ref,
    dp_ref,
    acc_ref,
    part_ref,
    rs_ref,
    sum_ref,
    full_ref,
    vec_ref,
    vdp_ref,
    vec2_ref,
    vz_ref,
    vec3_ref,
    vy_ref,
    p_send,
    p_recv,
    m_send,
    m_recv,
    s_send,
    s_recv,
    d_send,
    d_recv,
    rs_send,
    rs_recv,
    ag_send,
    ag_recv,
    v_send,
    v_recv,
    t_send,
    t_recv,
):
    core = lax.axis_index("dp")
    k = lax.axis_index("seq")
    head = lax.axis_index("head")
    y = over(k, RING)
    z = left_over(k, RING)
    right = lax.rem(k + 1, SEQ)
    left = lax.rem(k + SEQ - 1, SEQ)
    up = lax.rem(k + RING, SEQ)
    down = lax.rem(k + SEQ - RING, SEQ)

    peers = [{"dp": 1 - core}]
    peers += [{"seq": y * RING + lax.rem(z + d, RING)} for d in range(1, RING)]
    peers += [{"seq": lax.rem(y + d, ROWS) * RING + z} for d in range(1, ROWS)]
    peers += [{"head": lax.rem(head + d, HEADS_AX)} for d in range(1, HEADS_AX)]
    barrier = pltpu.get_barrier_semaphore()
    for peer in peers:
        pl.semaphore_signal(barrier, inc=1, device_id=peer, device_id_type=MESH)

    lens = len_ref[...].astype(F32)
    docs = lens.shape[1]
    sub, lane = iota((docs, docs), 0), iota((docs, docs), 1)
    lens_col = jnp.sum(jnp.where(sub == lane, lens, 0.0), axis=1, keepdims=True)
    ends_row = jnp.sum(jnp.where(sub <= lane, lens_col, 0.0), axis=0, keepdims=True)
    ends_col = jnp.sum(jnp.where(lane <= sub, lens, 0.0), axis=1, keepdims=True)
    anchor = k * TOK
    pos_c = (anchor + iota((TOK, docs), 0)).astype(F32)
    pos_r = (anchor + iota((docs, TOK), 1)).astype(F32)
    one_r = (anchor + iota((1, docs), 0)).astype(F32)
    doc_c = jnp.sum(jnp.where(ends_row <= pos_c, 1.0, 0.0), axis=1, keepdims=True)
    doc_r = jnp.sum(jnp.where(ends_col <= pos_r, 1.0, 0.0), axis=0, keepdims=True)
    before = jnp.sum(jnp.where(ends_row <= one_r - 1.0, 1.0, 0.0), axis=1, keepdims=True)
    before = jnp.where(one_r[:, :1] < 0.5, -1.0, before)
    last = jnp.sum(jnp.where(ends_row <= one_r + (TOK - 1.0), 1.0, 0.0), axis=1, keepdims=True)
    enter = jnp.where(doc_c == before, 1.0, 0.0)
    leave = jnp.where(doc_c == last, 1.0, 0.0)
    same_end = jnp.where(last == before, 1.0, 0.0)

    bq, cq = b_ref[...], c_ref[...]
    rows, cols = iota((TOK, TOK), 0), iota((TOK, TOK), 1)
    cm, bm = cq.astype(F32) * enter, bq.astype(F32) * leave
    cb_ref[0], cb_ref[1] = cm.astype(BF16), bm.astype(BF16)
    cbt_ref[0], cbt_ref[1] = cm.T.astype(BF16), bm.T.astype(BF16)

    hsub, hlane = iota((HEADS, HEADS), 0), iota((HEADS, HEADS), 1)
    rate_col = jnp.sum(jnp.where(hsub == hlane, rate_ref[...], 0.0), axis=1, keepdims=True)
    skip_col = jnp.sum(jnp.where(hsub == hlane, skip_ref[...], 0.0), axis=1, keepdims=True)
    step = step_ref[...]
    tri = jnp.where(rows >= cols, 1.0, 0.0).astype(BF16)
    owner = jnp.where(iota((HEADS, FEAT), 1) // HEAD_DIM == iota((HEADS, FEAT), 0), 1.0, 0.0)
    ob_ref[...] = owner.astype(BF16)
    skx_ref[...] = jnp.sum(owner * skip_col, axis=0, keepdims=True)
    running = sum(nt(tri, part) for part in split3(-(step * rate_col)))
    rt_ref[0], rt_ref[1], rt_ref[2] = split3(running)

    def remote(src, dst, send, recv, device):
        return pltpu.make_async_remote_copy(
            src_ref=src,
            dst_ref=dst,
            send_sem=send,
            recv_sem=recv,
            device_id=device,
            device_id_type=MESH,
        )

    pl.semaphore_wait(barrier, len(peers))
    passing = jnp.exp(running[TOK - 1 :, :]) * same_end
    wide = jnp.concatenate([passing, jnp.zeros((1, 128 - HEADS), F32)], axis=1)
    thz_ref[z] = jnp.broadcast_to(wide, (8, 128))

    def copy_t(d, slot):
        target = y * RING + lax.rem(z + d, RING)
        return remote(
            thz_ref.at[z], thz_ref.at[slot], t_send.at[d], t_recv.at[d], {"seq": target}
        )

    for d in range(1, RING):
        copy_t(d, z).start()

    def prepare(i):
        at = pl.ds(pl.multiple_of(i * WIDE, WIDE), WIDE)
        ob = ob_ref[:, at]
        rx = nn(rt_ref[0], ob) + nn(rt_ref[1], ob) + nn(rt_ref[2], ob)
        end = rx[TOK - 1 : TOK, :]
        mid = 0.5 * end
        em = jnp.exp(mid - rx)
        em_ref[:, at] = em
        x_f, dy_f = x_ref[:, at].astype(F32), dy_ref[:, at].astype(F32)
        sk_ref[:, at] = jnp.broadcast_to(jnp.sum(x_f * dy_f, axis=0, keepdims=True), (8, WIDE))
        xh, xl = split2(em * x_f)
        dyh, dyl = split2(jnp.exp(rx - mid) * dy_f)
        xh_ref[:, at], xl_ref[:, at], dyh_ref[:, at], dyl_ref[:, at] = xh, xl, dyh, dyl
        g = jnp.exp(mid)
        th = jnp.exp(end) * same_end
        local = g * (nn(cbt_ref[1], xh) + nn(cbt_ref[1], xl))
        local_d = g * (nn(cbt_ref[0], dyh) + nn(cbt_ref[0], dyl))
        for q in range(2):
            cut = slice(q * 128, q * 128 + 128)
            g_ref[2 * i + q] = jnp.broadcast_to(g[:, cut], (8, 128))
            th_ref[2 * i + q] = jnp.broadcast_to(th[:, cut], (8, 128))
            for n in range(PIECES):
                some = slice(n * HALF, n * HALF + HALF)
                l_ref[PER * i + PIECES * q + n] = local[some, cut]
                ld_ref[PER * i + PIECES * q + n] = local_d[some, cut]

    def make_weights():
        for d in range(1, RING):
            copy_t(d, lax.rem(z + RING - d, RING)).wait()
        ones = jnp.ones((8, 128), F32)
        ahead, behind = ones, ones
        for n in range(RING):
            ahead = ahead * jnp.where(n < z, thz_ref[n], ones)
            behind = behind * jnp.where(n > z, thz_ref[n], ones)
        pick = iota((8, 128), 0)
        row = ahead * behind * thz_ref[z]
        table = jnp.where(pick == 0, ahead, jnp.where(pick == 1, behind, row))
        table = sum(nn(part[:, :HEADS], ob_ref[...]) for part in split3(table))
        for n in range(FEAT // 128):
            w_ref[n] = table[:, n * 128 : (n + 1) * 128]

    def make_scores():
        same = doc_c == doc_r
        lower = same & (iota((TOK, TOK), 0) >= iota((TOK, TOK), 1))
        upper = same & (iota((TOK, TOK), 0) <= iota((TOK, TOK), 1))
        sm_ref[0], sm_ref[1] = split2(jnp.where(lower, nt(c_ref[...], b_ref[...]), 0.0))
        smt_ref[0], smt_ref[1] = split2(jnp.where(upper, nt(b_ref[...], c_ref[...]), 0.0))
        mask_ref[...] = jnp.where(lower, 1.0, 0.0)

    w_ref[...] = jnp.ones_like(w_ref)
    acc_ref[...] = jnp.zeros_like(acc_ref)
    rc_ref[...] = jnp.zeros_like(rc_ref)
    ds_ref[...] = jnp.zeros_like(ds_ref)

    def copy_p(s):
        return remote(send_p.at[s], recv_p.at[s], p_send.at[s], p_recv.at[s], {"seq": right})

    def copy_m(s):
        return remote(send_m.at[s], recv_m.at[s], m_send.at[s], m_recv.at[s], {"seq": left})

    def copy_s(s):
        return remote(ysend_s.at[s], cin_s.at[s], s_send.at[s], s_recv.at[s], {"seq": up})

    def copy_d(s):
        return remote(ysend_d.at[s], cin_d.at[s], d_send.at[s], d_recv.at[s], {"seq": down})

    def weights(s):
        fb = over(s, PIECES)
        return th_ref[fb, 0:1], w_ref[fb, 0:1], w_ref[fb, 1:2], w_ref[fb, 2:3]

    def chain(s, first, final, copy, recv, send, mine, other, cin_mine, cin_other, forward):
        th, ahead, behind, _ = weights(s)
        weight = ahead if forward else behind

        @pl.when(first)
        def _():
            recv[s] = jnp.zeros((2 * HALF, 128), F32)

        @pl.when(jnp.logical_not(first))
        def _():
            copy(s).wait_recv()

        @pl.when(s < LATE)
        def _():
            send[s, :HALF] = th * recv[s, :HALF] + mine[s]
            send[s, HALF:] = recv[s, HALF:] + weight * other[s]

        @pl.when(s >= LATE)
        def _():
            send[s, :HALF] = th * (recv[s, :HALF] + weight * cin_mine[s]) + mine[s]
            send[s, HALF:] = recv[s, HALF:] + cin_other[s]

        @pl.when(jnp.logical_not(final))
        def _():
            copy(s).start()

    def pass_on(s, has_recv, has_send, copy, cin, ysend, total):
        @pl.when(has_recv)
        def _():
            copy(s).wait_recv()

        @pl.when(jnp.logical_not(has_recv))
        def _():
            cin[s] = jnp.zeros((HALF, 128), F32)

        @pl.when(has_send)
        def _():
            ysend[s] = total(s) + weights(s)[3] * cin[s]
            copy(s).start()

    def pass_s(s, total):
        pass_on(s, y > 0, y < ROWS - 1, copy_s, cin_s, ysend_s, total)

    def pass_d(s, total):
        pass_on(s, y < ROWS - 1, y > 0, copy_d, cin_d, ysend_d, total)

    def keep(s, state, cin, dest):
        cin[s] = state
        dest[0, s], dest[1, s] = split2(state * g_ref[over(s, PIECES), 0:1])

    def own_heads(i):
        shape = (WIDE, 128)
        hit = iota(shape, 0) // HEAD_DIM + 4 * i == iota(shape, 1)
        return jnp.where(hit, 1.0, 0.0).astype(BF16)

    def add_products(i, at, y_part, dx_part, extra):
        dyp = dyh_ref[:, at].astype(F32) + dyl_ref[:, at].astype(F32)
        xp = xh_ref[:, at].astype(F32) + xl_ref[:, at].astype(F32)
        prod = dyp * y_part - xp * dx_part
        if extra is not None:
            prod = prod + jnp.where(iota((TOK, WIDE), 0) == TOK - 1, extra, 0.0)
        heads = own_heads(i)
        rc_ref[...] += sum(nn(part, heads) for part in split3(prod))

    def local_work(i, turn):
        at = pl.ds(pl.multiple_of(i * WIDE, WIDE), WIDE)

        @pl.when(turn == 0)
        def _():
            yl_ref[...] = (
                nn(sm_ref[0], xh_ref[:, at])
                + nn(sm_ref[0], xl_ref[:, at])
                + nn(sm_ref[1], xh_ref[:, at])
            )

        @pl.when(turn == 1)
        def _():
            dx_ref[:, at] = (
                nn(smt_ref[0], dyh_ref[:, at])
                + nn(smt_ref[0], dyl_ref[:, at])
                + nn(smt_ref[1], dyh_ref[:, at])
            )

        @pl.when(turn == 2)
        def _():
            add_products(i, at, yl_ref[...], dx_ref[:, at], None)

        @pl.when(turn == 3)
        def _():
            ds_ref[...] += (
                nt(dyh_ref[:, at], xh_ref[:, at])
                + nt(dyh_ref[:, at], xl_ref[:, at])
                + nt(dyl_ref[:, at], xh_ref[:, at])
            )

    def states(ref, part, i):
        def column(q):
            some = [ref[part, PER * i + PIECES * q + n] for n in range(PIECES)]
            return jnp.concatenate(some, axis=0)

        return jnp.concatenate([column(0), column(1)], axis=1)

    def grads(i):
        at = pl.ds(pl.multiple_of(i * WIDE, WIDE), WIDE)
        sh, sl = states(sp_ref, 0, i), states(sp_ref, 1, i)
        dh, dl = states(dp_ref, 0, i), states(dp_ref, 1, i)
        xh, xl, dyh, dyl = xh_ref[:, at], xl_ref[:, at], dyh_ref[:, at], dyl_ref[:, at]
        acc_ref[:, :STATE] += nt(xh, dh) + nt(xl, dh) + nt(xh, dl)
        acc_ref[:, STATE:] += nt(dyh, sh) + nt(dyl, sh) + nt(dyh, sl)
        y_part = nn(cb_ref[0], sh) + nn(cb_ref[0], sl)
        dx_part = nn(cb_ref[1], dh) + nn(cb_ref[1], dl)
        ends = []
        for q in range(2):
            total = 0.0
            for n in range(PIECES):
                s = PER * i + PIECES * q + n
                out = th_ref[2 * i + q, 0:1] * cin_s[s] + l_ref[s]
                total = total + jnp.sum(out * cin_d[s], axis=0, keepdims=True)
            ends.append(total)
        add_products(i, at, y_part, dx_part, jnp.concatenate(ends, axis=1))
        whole = em_ref[:, at] * (dx_ref[:, at] + dx_part)
        whole = whole + skx_ref[:, at] * dy_ref[:, at].astype(F32)
        gx_ref[:, at] = whole.astype(BF16)

    far = HOP * jnp.maximum(z, RING - 1 - z)
    hops_s, hops_d = y, ROWS - 1 - y

    def slot_body(number, _):
        tau = number - 1

        @pl.when(tau == 2)
        def _():
            make_weights()

        def at(n, low, high, work):
            @pl.when((n >= low) & (n < high))
            def _():
                work(n)

        def forward(s):
            chain(
                s, z == 0, z == RING - 1, copy_p, recv_p, send_p, l_ref, ld_ref, cin_s, cin_d, True
            )

        def backward(s):
            chain(
                s, z == RING - 1, z == 0, copy_m, recv_m, send_m, ld_ref, l_ref, cin_d, cin_s, False
            )

        at(tau - HOP * z, 0, SLICES, forward)
        at(tau - HOP * (RING - 1 - z), 0, SLICES, backward)

        def early_s(s):
            pass_s(s, lambda s: weights(s)[2] * l_ref[s])

        def early_d(s):
            pass_d(s, lambda s: weights(s)[1] * ld_ref[s])

        at(tau + LATE - DELAY - LAG * hops_s, LATE, SLICES, early_s)
        at(tau + LATE - DELAY - LAG * hops_d, LATE, SLICES, early_d)

        def late_s(s):
            pass_s(s, lambda s: weights(s)[2] * send_p[s, :HALF] + recv_m[s, HALF:])
            keep(s, recv_p[s, :HALF] + weights(s)[1] * cin_s[s], cin_s, sp_ref)

        def late_d(s):
            pass_d(s, lambda s: weights(s)[1] * send_m[s, :HALF] + recv_p[s, HALF:])
            keep(s, recv_m[s, :HALF] + weights(s)[2] * cin_d[s], cin_d, dp_ref)

        at(tau - far - LAG * hops_s, 0, LATE, late_s)
        at(tau - far - LAG * hops_d, 0, LATE, late_d)

        def whole(s):
            _, ahead, behind, _ = weights(s)
            state = recv_p[s, :HALF] + ahead * (cin_s[s] + recv_m[s, HALF:])
            state_d = recv_m[s, :HALF] + behind * (cin_d[s] + recv_p[s, HALF:])
            keep(s, state, cin_s, sp_ref)
            keep(s, state_d, cin_d, dp_ref)

        at(tau - far, LATE, SLICES, whole)

        @pl.when(tau == 0)
        def _():
            make_scores()

        beat = PER // 2
        place = over(tau + beat, beat)

        @pl.when((tau == -1) | ((left_over(tau + beat, beat) == 0) & (place < GROUPS)))
        def _():
            chosen = 0
            for n in range(1, GROUPS):
                chosen = jnp.where((tau >= 0) & (place == n), ORDER[n], chosen)
            prepare(chosen)

        turn = left_over(tau, PER)

        @pl.when((tau >= PER) & (tau < SLICES + PER) & (left_over(turn, PIECES // 2) == 0))
        def _():
            local_work(over(tau, PER) - 1, over(turn, PIECES // 2))

        def both(c, _):
            done = jnp.where(c == 0, tau - far - LAG * jnp.maximum(hops_s, hops_d), tau - far)
            done = done - (PER - 1)
            low = jnp.where(c == 0, 0, LATE)
            high = jnp.where(c == 0, LATE, SLICES)

            @pl.when((done >= low) & (done < high) & (left_over(done, PER) == 0))
            def _():
                grads(over(done, PER))

            return 0

        lax.fori_loop(0, 2, both, 0)
        return 0

    lax.fori_loop(0, SLOTS + 1, slot_body, 0)

    d_scores = jnp.where(mask_ref[...] > 0.5, ds_ref[...], 0.0)
    bq, cq = b_ref[...], c_ref[...]
    sh, sl = split2(d_scores)
    th, tl = split2(d_scores.T)
    part_ref[:, :STATE] = leave * acc_ref[:, :STATE] + nn(th, cq) + nn(tl, cq)
    part_ref[:, STATE:] = enter * acc_ref[:, STATE:] + nn(sh, bq) + nn(sl, bq)
    quarter = TOK // HEADS_AX

    def copy_rs(d):
        target = lax.rem(head + d, HEADS_AX)
        rows_of = pl.ds(pl.multiple_of(target * quarter, quarter), quarter)
        return remote(
            part_ref.at[rows_of], rs_ref.at[d], rs_send.at[d], rs_recv.at[d], {"head": target}
        )

    def copy_ag(d):
        target = lax.rem(head + d, HEADS_AX)
        return remote(
            sum_ref, full_ref.at[head], ag_send.at[d], ag_recv.at[d], {"head": target}
        )

    def wait_ag(d):
        source = lax.rem(head + HEADS_AX - d, HEADS_AX)
        target = lax.rem(head + d, HEADS_AX)
        return remote(
            sum_ref, full_ref.at[source], ag_send.at[d], ag_recv.at[d], {"head": target}
        )

    for d in range(1, HEADS_AX):
        copy_rs(d).start()

    tri = jnp.where(iota((TOK, TOK), 0) >= iota((TOK, TOK), 1), 1.0, 0.0).astype(BF16)
    dl = sum(nn(part[:HEADS], tri) for part in split3(rc_ref[...].T))
    gs_ref[...] = -(rate_col * dl)
    rate_part = -jnp.sum(step * dl, axis=1, keepdims=True)
    skip_part = sum(nt(ob_ref[...], part) for part in split3(sk_ref[...]))[:, :1]
    diag = iota((HEADS, 128), 0) == iota((HEADS, 128), 1)
    rate_row = jnp.sum(jnp.where(diag, rate_part, 0.0), axis=0, keepdims=True)
    skip_row = jnp.sum(jnp.where(diag, skip_part, 0.0), axis=0, keepdims=True)
    first = iota((8, 128), 0)
    vec_ref[...] = jnp.where(first == 0, rate_row, jnp.where(first == 1, skip_row, 0.0))

    swap = remote(vec_ref, vdp_ref, v_send.at[0], v_recv.at[0], {"dp": 1 - core})
    swap.start()
    swap.wait()
    vec2_ref[...] = vec_ref[...] + vdp_ref[...]
    vz_ref[z] = vec2_ref[...]

    def copy_z(d, slot):
        target = y * RING + lax.rem(z + d, RING)
        return remote(vec2_ref, vz_ref.at[slot], v_send.at[d], v_recv.at[d], {"seq": target})

    for d in range(1, RING):
        copy_z(d, z).start()
    mine_rows = pl.ds(pl.multiple_of(head * quarter, quarter), quarter)
    for d in range(1, HEADS_AX):
        copy_rs(d).wait()
    sum_ref[...] = part_ref[mine_rows] + rs_ref[1] + rs_ref[2] + rs_ref[3]
    full_ref[head] = sum_ref[...]
    for d in range(1, HEADS_AX):
        copy_ag(d).start()

    for d in range(1, RING):
        copy_z(d, lax.rem(z + RING - d, RING)).wait()
    vec3_ref[...] = sum(vz_ref[n] for n in range(RING))
    vy_ref[y] = vec3_ref[...]

    def copy_y(d, slot):
        target = lax.rem(y + d, ROWS) * RING + z
        n = RING + d
        return remote(vec3_ref, vy_ref.at[slot], v_send.at[n], v_recv.at[n], {"seq": target})

    for d in range(1, ROWS):
        copy_y(d, y).start()
    for d in range(1, HEADS_AX):
        wait_ag(d).wait()
    for n in range(HEADS_AX):
        gb_ref[n * quarter : (n + 1) * quarter] = full_ref[n, :, :STATE]
        gc_ref[n * quarter : (n + 1) * quarter] = full_ref[n, :, STATE:]
    for d in range(1, ROWS):
        copy_y(d, lax.rem(y + ROWS - d, ROWS)).wait()
    whole_vec = sum(vy_ref[n] for n in range(ROWS))
    gr_ref[...] = whole_vec[0:1, :HEADS]
    gk_ref[...] = whole_vec[1:2, :HEADS]

    def drain(s, _):
        @pl.when(z < RING - 1)
        def _():
            copy_p(s).wait_send()

        @pl.when(z > 0)
        def _():
            copy_m(s).wait_send()

        @pl.when(y < ROWS - 1)
        def _():
            copy_s(s).wait_send()

        @pl.when(y > 0)
        def _():
            copy_d(s).wait_send()

        return 0

    lax.fori_loop(0, SLICES, drain, 0)


def hand_out(*refs):
    count = len(refs) // 2
    for n in range(count):
        refs[count + n][...] = refs[n][...]


def on_device(inputs, proj_b, proj_c, step_size, decay_rate, skip_gain, doc_lengths, grad_out):
    vmem = pl.BlockSpec(memory_space=pltpu.VMEM)
    state = pltpu.VMEM((SLICES, HALF, 128), F32)
    message = pltpu.VMEM((SLICES, 2 * HALF, 128), F32)
    pair = pltpu.VMEM((2, SLICES, HALF, 128), BF16)
    sems = pltpu.SemaphoreType.DMA((SLICES,))
    tile = pltpu.VMEM((8, 128), F32)
    quarter = TOK // HEADS_AX
    scratch = [
        pltpu.VMEM((TOK, FEAT), BF16),
        pltpu.VMEM((TOK, FEAT), BF16),
        pltpu.VMEM((TOK, FEAT), BF16),
        pltpu.VMEM((TOK, FEAT), BF16),
        pltpu.VMEM((TOK, FEAT), F32),
        pltpu.VMEM((TOK, FEAT), F32),
        pltpu.VMEM((TOK, WIDE), F32),
        pltpu.VMEM((HEADS, FEAT), BF16),
        pltpu.VMEM((3, TOK, HEADS), BF16),
        pltpu.VMEM((2, TOK, TOK), BF16),
        pltpu.VMEM((2, TOK, TOK), BF16),
        pltpu.VMEM((TOK, TOK), F32),
        pltpu.VMEM((2, TOK, STATE), BF16),
        pltpu.VMEM((2, STATE, TOK), BF16),
        pltpu.VMEM((FEAT // 128, 8, 128), F32),
        pltpu.VMEM((FEAT // 128, 8, 128), F32),
        pltpu.VMEM((FEAT // 128, 8, 128), F32),
        pltpu.VMEM((RING, 8, 128), F32),
        pltpu.VMEM((TOK, TOK), F32),
        pltpu.VMEM((1, FEAT), F32),
        pltpu.VMEM((8, FEAT), F32),
        pltpu.VMEM((TOK, 128), F32),
        state,
        state,
        message,
        message,
        message,
        message,
        state,
        state,
        state,
        state,
        pair,
        pair,
        pltpu.VMEM((TOK, 2 * STATE), F32),
        pltpu.VMEM((TOK, 2 * STATE), F32),
        pltpu.VMEM((HEADS_AX, quarter, 2 * STATE), F32),
        pltpu.VMEM((quarter, 2 * STATE), F32),
        pltpu.VMEM((HEADS_AX, quarter, 2 * STATE), F32),
        tile,
        tile,
        tile,
        pltpu.VMEM((RING, 8, 128), F32),
        tile,
        pltpu.VMEM((ROWS, 8, 128), F32),
        sems,
        sems,
        sems,
        sems,
        sems,
        sems,
        sems,
        sems,
        pltpu.SemaphoreType.DMA((HEADS_AX,)),
        pltpu.SemaphoreType.DMA((HEADS_AX,)),
        pltpu.SemaphoreType.DMA((HEADS_AX,)),
        pltpu.SemaphoreType.DMA((HEADS_AX,)),
        pltpu.SemaphoreType.DMA((RING + ROWS,)),
        pltpu.SemaphoreType.DMA((RING + ROWS,)),
        pltpu.SemaphoreType.DMA((RING,)),
        pltpu.SemaphoreType.DMA((RING,)),
    ]
    shapes = (
        jax.ShapeDtypeStruct((TOK, FEAT), BF16),
        jax.ShapeDtypeStruct((TOK, STATE), F32),
        jax.ShapeDtypeStruct((TOK, STATE), F32),
        jax.ShapeDtypeStruct((HEADS, TOK), F32),
        jax.ShapeDtypeStruct((1, HEADS), F32),
        jax.ShapeDtypeStruct((1, HEADS), F32),
    )
    results = pl.pallas_call(
        kernel,
        out_shape=shapes,
        in_specs=[vmem] * 8,
        out_specs=(vmem,) * 6,
        scratch_shapes=scratch,
        compiler_params=pltpu.CompilerParams(
            collective_id=0, has_side_effects=True, vmem_limit_bytes=56 << 20
        ),
    )(
        inputs[0],
        grad_out[0],
        proj_b[0],
        proj_c[0],
        step_size[0],
        decay_rate[None],
        skip_gain[None],
        doc_lengths,
    )
    grad_x, grad_b, grad_c, grad_step, grad_rate, grad_skip = pl.pallas_call(
        hand_out,
        out_shape=shapes,
        in_specs=[vmem] * 6,
        out_specs=(vmem,) * 6,
        compiler_params=pltpu.CompilerParams(vmem_limit_bytes=56 << 20),
    )(*results)
    return (
        grad_x[None],
        grad_b[None],
        grad_c[None],
        grad_step[None],
        grad_rate[0],
        grad_skip[0],
    )


def solution(mesh):
    in_specs = (
        P("dp", "seq", "head"),
        P("dp", "seq", None),
        P("dp", "seq", None),
        P("dp", "head", "seq"),
        P("head"),
        P("head"),
        P("dp", None),
        P("dp", "seq", "head"),
    )
    out_specs = (
        P("dp", "seq", "head"),
        P("dp", "seq", None),
        P("dp", "seq", None),
        P("dp", "head", "seq"),
        P("head"),
        P("head"),
    )
    return jax.shard_map(
        on_device, mesh=mesh, in_specs=in_specs, out_specs=out_specs, check_vma=False
    )
```

```python
import jax
import jax.numpy as jnp
from jax import lax
from jax.experimental import pallas as pl
from jax.experimental.pallas import tpu as pltpu
from jax.sharding import PartitionSpec as P

F32 = jnp.float32
BF16 = jnp.bfloat16
MESH = pl.DeviceIdType.MESH

ROWS = 4
RING = 8
SEQ = ROWS * RING
HEADS_AX = 4
TOK = 256
HEADS = 32
HEAD_DIM = 64
STATE = 128
FEAT = HEADS * HEAD_DIM
WIDE = 256
GROUPS = FEAT // WIDE
PIECES = 2
PER = 2 * PIECES
SLICES = PER * GROUPS
HALF = STATE // PIECES
LATE = SLICES // 2
HOP = 11 * PIECES // 2
LAG = 3 * PIECES // 2
DELAY = PER + 2
SLOTS = HOP * (RING - 1) // 4 + SLICES
ORDER = (0, 1, 4, 2, 5, 3, 6, 7)
READY = 2


def nn(a, b):
    return lax.dot_general(a, b, (((1,), (0,)), ((), ())), preferred_element_type=F32)


def nt(a, b):
    return lax.dot_general(a, b, (((1,), (1,)), ((), ())), preferred_element_type=F32)


def split2(value):
    high = value.astype(BF16)
    return high, (value - high.astype(F32)).astype(BF16)


def split3(value):
    high = value.astype(BF16)
    rest = value - high.astype(F32)
    middle = rest.astype(BF16)
    return high, middle, (rest - middle.astype(F32)).astype(BF16)


def over(n, size):
    return lax.shift_right_arithmetic(n, jnp.int32(size.bit_length() - 1))


def left_over(n, size):
    return lax.bitwise_and(n, jnp.int32(size - 1))


def iota(shape, dim):
    return lax.broadcasted_iota(jnp.int32, shape, dim)


def kernel(
    x_hbm,
    dy_hbm,
    b_ref,
    c_ref,
    step_ref,
    rate_ref,
    skip_ref,
    len_ref,
    gx_ref,
    gb_ref,
    gc_ref,
    gs_ref,
    gr_ref,
    gk_ref,
    x_ref,
    dy_ref,
    xh_ref,
    xl_ref,
    dyh_ref,
    dyl_ref,
    em_ref,
    dx_ref,
    yl_ref,
    ob_ref,
    rt_ref,
    sm_ref,
    smt_ref,
    ds_ref,
    cb_ref,
    cbt_ref,
    g_ref,
    th_ref,
    w_ref,
    thz_ref,
    mask_ref,
    skx_ref,
    sk_ref,
    rc_ref,
    l_ref,
    ld_ref,
    recv_p,
    recv_m,
    send_p,
    send_m,
    cin_s,
    cin_d,
    ysend_s,
    ysend_d,
    sp_ref,
    dp_ref,
    acc_ref,
    part_ref,
    rs_ref,
    sum_ref,
    full_ref,
    vec_ref,
    vdp_ref,
    vec2_ref,
    vz_ref,
    vec3_ref,
    vy_ref,
    p_send,
    p_recv,
    m_send,
    m_recv,
    s_send,
    s_recv,
    d_send,
    d_recv,
    rs_send,
    rs_recv,
    ag_send,
    ag_recv,
    v_send,
    v_recv,
    t_send,
    t_recv,
    in_sems,
):
    core = lax.axis_index("dp")
    k = lax.axis_index("seq")
    head = lax.axis_index("head")
    y = over(k, RING)
    z = left_over(k, RING)
    right = lax.rem(k + 1, SEQ)
    left = lax.rem(k + SEQ - 1, SEQ)
    up = lax.rem(k + RING, SEQ)
    down = lax.rem(k + SEQ - RING, SEQ)

    peers = [{"dp": 1 - core}]
    peers += [{"seq": y * RING + lax.rem(z + d, RING)} for d in range(1, RING)]
    peers += [{"seq": lax.rem(y + d, ROWS) * RING + z} for d in range(1, ROWS)]
    peers += [{"head": lax.rem(head + d, HEADS_AX)} for d in range(1, HEADS_AX)]
    barrier = pltpu.get_barrier_semaphore()
    for peer in peers:
        pl.semaphore_signal(barrier, inc=1, device_id=peer, device_id_type=MESH)

    load_x = pltpu.make_async_copy(x_hbm, x_ref, in_sems.at[0])
    load_dy = pltpu.make_async_copy(dy_hbm, dy_ref, in_sems.at[1])
    load_x.start()
    load_dy.start()

    lens = len_ref[...].astype(F32)
    docs = lens.shape[1]
    sub, lane = iota((docs, docs), 0), iota((docs, docs), 1)
    lens_col = jnp.sum(jnp.where(sub == lane, lens, 0.0), axis=1, keepdims=True)
    ends_row = jnp.sum(jnp.where(sub <= lane, lens_col, 0.0), axis=0, keepdims=True)
    ends_col = jnp.sum(jnp.where(lane <= sub, lens, 0.0), axis=1, keepdims=True)
    anchor = k * TOK
    pos_c = (anchor + iota((TOK, docs), 0)).astype(F32)
    pos_r = (anchor + iota((docs, TOK), 1)).astype(F32)
    one_r = (anchor + iota((1, docs), 0)).astype(F32)
    doc_c = jnp.sum(jnp.where(ends_row <= pos_c, 1.0, 0.0), axis=1, keepdims=True)
    doc_r = jnp.sum(jnp.where(ends_col <= pos_r, 1.0, 0.0), axis=0, keepdims=True)
    before = jnp.sum(jnp.where(ends_row <= one_r - 1.0, 1.0, 0.0), axis=1, keepdims=True)
    before = jnp.where(one_r[:, :1] < 0.5, -1.0, before)
    last = jnp.sum(jnp.where(ends_row <= one_r + (TOK - 1.0), 1.0, 0.0), axis=1, keepdims=True)
    enter = jnp.where(doc_c == before, 1.0, 0.0)
    leave = jnp.where(doc_c == last, 1.0, 0.0)
    same_end = jnp.where(last == before, 1.0, 0.0)

    bq, cq = b_ref[...], c_ref[...]
    rows, cols = iota((TOK, TOK), 0), iota((TOK, TOK), 1)
    cm, bm = cq.astype(F32) * enter, bq.astype(F32) * leave
    cb_ref[0], cb_ref[1] = cm.astype(BF16), bm.astype(BF16)
    cbt_ref[0], cbt_ref[1] = cm.T.astype(BF16), bm.T.astype(BF16)

    hsub, hlane = iota((HEADS, HEADS), 0), iota((HEADS, HEADS), 1)
    rate_col = jnp.sum(jnp.where(hsub == hlane, rate_ref[...], 0.0), axis=1, keepdims=True)
    skip_col = jnp.sum(jnp.where(hsub == hlane, skip_ref[...], 0.0), axis=1, keepdims=True)
    step = step_ref[...]
    tri = jnp.where(rows >= cols, 1.0, 0.0).astype(BF16)
    owner = jnp.where(over(iota((HEADS, FEAT), 1), HEAD_DIM) == iota((HEADS, FEAT), 0), 1.0, 0.0)
    ob_ref[...] = owner.astype(BF16)
    skx_ref[...] = jnp.sum(owner * skip_col, axis=0, keepdims=True)
    running = sum(nt(tri, part) for part in split3(-(step * rate_col)))
    rt_ref[0], rt_ref[1], rt_ref[2] = split3(running)

    def remote(src, dst, send, recv, device):
        return pltpu.make_async_remote_copy(
            src_ref=src,
            dst_ref=dst,
            send_sem=send,
            recv_sem=recv,
            device_id=device,
            device_id_type=MESH,
        )

    passing = jnp.exp(running[TOK - 1 :, :]) * same_end
    wide = jnp.concatenate([passing, jnp.zeros((1, 128 - HEADS), F32)], axis=1)
    thz_ref[z] = jnp.broadcast_to(wide, (8, 128))

    def copy_t(d, slot):
        target = y * RING + lax.rem(z + d, RING)
        return remote(
            thz_ref.at[z], thz_ref.at[slot], t_send.at[d], t_recv.at[d], {"seq": target}
        )

    def prepare(i):
        at = pl.ds(pl.multiple_of(i * WIDE, WIDE), WIDE)
        ob = ob_ref[:, at]
        rx = nn(rt_ref[0], ob) + nn(rt_ref[1], ob) + nn(rt_ref[2], ob)
        end = rx[TOK - 1 : TOK, :]
        mid = 0.5 * end
        em = jnp.exp(mid - rx)
        em_ref[:, at] = em
        x_f, dy_f = x_ref[:, at].astype(F32), dy_ref[:, at].astype(F32)
        sk_ref[:, at] = jnp.broadcast_to(jnp.sum(x_f * dy_f, axis=0, keepdims=True), (8, WIDE))
        xh, xl = split2(em * x_f)
        dyh, dyl = split2(jnp.exp(rx - mid) * dy_f)
        xh_ref[:, at], xl_ref[:, at], dyh_ref[:, at], dyl_ref[:, at] = xh, xl, dyh, dyl
        g = jnp.exp(mid)
        th = jnp.exp(end) * same_end
        local = g * (nn(cbt_ref[1], xh) + nn(cbt_ref[1], xl))
        local_d = g * (nn(cbt_ref[0], dyh) + nn(cbt_ref[0], dyl))
        for q in range(2):
            cut = slice(q * 128, q * 128 + 128)
            g_ref[2 * i + q] = jnp.broadcast_to(g[:, cut], (8, 128))
            th_ref[2 * i + q] = jnp.broadcast_to(th[:, cut], (8, 128))
            for n in range(PIECES):
                some = slice(n * HALF, n * HALF + HALF)
                l_ref[PER * i + PIECES * q + n] = local[some, cut]
                ld_ref[PER * i + PIECES * q + n] = local_d[some, cut]

    def choose(place):
        chosen = 0
        for n in range(1, GROUPS):
            chosen = jnp.where(place == n, ORDER[n], chosen)
        return chosen

    def prepare_next(place, _):
        prepare(choose(place))
        return 0

    load_x.wait()
    load_dy.wait()
    lax.fori_loop(0, READY, prepare_next, 0)
    pl.semaphore_wait(barrier, len(peers))
    for d in range(1, RING):
        copy_t(d, z).start()

    def make_weights():
        for d in range(1, RING):
            copy_t(d, lax.rem(z + RING - d, RING)).wait()
        ones = jnp.ones((8, 128), F32)
        ahead, behind = ones, ones
        for n in range(RING):
            ahead = ahead * jnp.where(n < z, thz_ref[n], ones)
            behind = behind * jnp.where(n > z, thz_ref[n], ones)
        pick = iota((8, 128), 0)
        row = ahead * behind * thz_ref[z]
        table = jnp.where(pick == 0, ahead, jnp.where(pick == 1, behind, row))
        table = sum(nn(part[:, :HEADS], ob_ref[...]) for part in split3(table))
        for n in range(FEAT // 128):
            w_ref[n] = table[:, n * 128 : (n + 1) * 128]

    def make_scores():
        same = doc_c == doc_r
        lower = same & (iota((TOK, TOK), 0) >= iota((TOK, TOK), 1))
        upper = same & (iota((TOK, TOK), 0) <= iota((TOK, TOK), 1))
        sm_ref[0], sm_ref[1] = split2(jnp.where(lower, nt(c_ref[...], b_ref[...]), 0.0))
        smt_ref[0], smt_ref[1] = split2(jnp.where(upper, nt(b_ref[...], c_ref[...]), 0.0))
        mask_ref[...] = jnp.where(lower, 1.0, 0.0)

    w_ref[...] = jnp.ones_like(w_ref)
    acc_ref[...] = jnp.zeros_like(acc_ref)
    rc_ref[...] = jnp.zeros_like(rc_ref)
    ds_ref[...] = jnp.zeros_like(ds_ref)

    def copy_p(part, s):
        return remote(
            send_p.at[part, s],
            recv_p.at[part, s],
            p_send.at[part, s],
            p_recv.at[part, s],
            {"seq": right},
        )

    def copy_m(part, s):
        return remote(
            send_m.at[part, s],
            recv_m.at[part, s],
            m_send.at[part, s],
            m_recv.at[part, s],
            {"seq": left},
        )

    def copy_s(s):
        return remote(ysend_s.at[s], cin_s.at[s], s_send.at[s], s_recv.at[s], {"seq": up})

    def copy_d(s):
        return remote(ysend_d.at[s], cin_d.at[s], d_send.at[s], d_recv.at[s], {"seq": down})

    def weights(s):
        fb = over(s, PIECES)
        return th_ref[fb, 0:1], w_ref[fb, 0:1], w_ref[fb, 1:2], w_ref[fb, 2:3]

    def chain(part, s, first, final, copy, recv, send, make):
        @pl.when(first)
        def _():
            recv[part, s] = jnp.zeros((HALF, 128), F32)

        @pl.when(jnp.logical_not(first))
        def _():
            copy(part, s).wait_recv()

        for late in range(2):

            @pl.when(s >= LATE if late else s < LATE)
            def _():
                send[part, s] = make(late, recv[part, s])

        @pl.when(jnp.logical_not(final))
        def _():
            copy(part, s).start()

    def pass_on(s, has_recv, has_send, copy, cin, ysend, total):
        @pl.when(has_recv)
        def _():
            copy(s).wait_recv()

        @pl.when(jnp.logical_not(has_recv))
        def _():
            cin[s] = jnp.zeros((HALF, 128), F32)

        @pl.when(has_send)
        def _():
            ysend[s] = total(s) + weights(s)[3] * cin[s]
            copy(s).start()

    def pass_s(s, total):
        pass_on(s, y > 0, y < ROWS - 1, copy_s, cin_s, ysend_s, total)

    def pass_d(s, total):
        pass_on(s, y < ROWS - 1, y > 0, copy_d, cin_d, ysend_d, total)

    def keep(s, state, cin, dest):
        cin[s] = state
        dest[0, s], dest[1, s] = split2(state * g_ref[over(s, PIECES), 0:1])

    def own_heads(i):
        shape = (WIDE, 128)
        hit = over(iota(shape, 0), HEAD_DIM) + 4 * i == iota(shape, 1)
        return jnp.where(hit, 1.0, 0.0).astype(BF16)

    def add_products(i, at, y_part, dx_part, extra):
        dyp = dyh_ref[:, at].astype(F32) + dyl_ref[:, at].astype(F32)
        xp = xh_ref[:, at].astype(F32) + xl_ref[:, at].astype(F32)
        prod = dyp * y_part - xp * dx_part
        if extra is not None:
            prod = prod + jnp.where(iota((TOK, WIDE), 0) == TOK - 1, extra, 0.0)
        heads = own_heads(i)
        rc_ref[...] += sum(nn(part, heads) for part in split3(prod))

    def local_work(i, turn):
        at = pl.ds(pl.multiple_of(i * WIDE, WIDE), WIDE)

        @pl.when(turn == 0)
        def _():
            yl_ref[...] = (
                nn(sm_ref[0], xh_ref[:, at])
                + nn(sm_ref[0], xl_ref[:, at])
                + nn(sm_ref[1], xh_ref[:, at])
            )

        @pl.when(turn == 1)
        def _():
            dx_ref[:, at] = (
                nn(smt_ref[0], dyh_ref[:, at])
                + nn(smt_ref[0], dyl_ref[:, at])
                + nn(smt_ref[1], dyh_ref[:, at])
            )

        @pl.when(turn == 2)
        def _():
            add_products(i, at, yl_ref[...], dx_ref[:, at], None)

        @pl.when(turn == 3)
        def _():
            ds_ref[...] += (
                nt(dyh_ref[:, at], xh_ref[:, at])
                + nt(dyh_ref[:, at], xl_ref[:, at])
                + nt(dyl_ref[:, at], xh_ref[:, at])
            )

    def states(ref, part, i):
        def column(q):
            some = [ref[part, PER * i + PIECES * q + n] for n in range(PIECES)]
            return jnp.concatenate(some, axis=0)

        return jnp.concatenate([column(0), column(1)], axis=1)

    def grads(i):
        at = pl.ds(pl.multiple_of(i * WIDE, WIDE), WIDE)
        sh, sl = states(sp_ref, 0, i), states(sp_ref, 1, i)
        dh, dl = states(dp_ref, 0, i), states(dp_ref, 1, i)
        xh, xl, dyh, dyl = xh_ref[:, at], xl_ref[:, at], dyh_ref[:, at], dyl_ref[:, at]
        acc_ref[:, :STATE] += nt(xh, dh) + nt(xl, dh) + nt(xh, dl)
        acc_ref[:, STATE:] += nt(dyh, sh) + nt(dyl, sh) + nt(dyh, sl)
        y_part = nn(cb_ref[0], sh) + nn(cb_ref[0], sl)
        dx_part = nn(cb_ref[1], dh) + nn(cb_ref[1], dl)
        ends = []
        for q in range(2):
            total = 0.0
            for n in range(PIECES):
                s = PER * i + PIECES * q + n
                out = th_ref[2 * i + q, 0:1] * cin_s[s] + l_ref[s]
                total = total + jnp.sum(out * cin_d[s], axis=0, keepdims=True)
            ends.append(total)
        add_products(i, at, y_part, dx_part, jnp.concatenate(ends, axis=1))
        whole = em_ref[:, at] * (dx_ref[:, at] + dx_part)
        whole = whole + skx_ref[:, at] * dy_ref[:, at].astype(F32)
        gx_ref[:, at] = whole.astype(BF16)

    from_left = over(HOP * z, 4)
    from_right = over(HOP * (RING - 1 - z), 4)
    far = jnp.maximum(from_left, from_right)
    need = jnp.where((z == 0) | (z == RING - 1), DELAY, over(HOP, 4))
    hops_s, hops_d = y, ROWS - 1 - y

    def slot_body(tau, _):
        def at(n, low, high, work):
            @pl.when((n >= low) & (n < high))
            def _():
                work(n)

        def run(forward, part, s):
            th, ahead, behind, _ = weights(s)
            weight = ahead if forward else behind
            mine, other = (l_ref, ld_ref) if forward else (ld_ref, l_ref)
            cin_mine, cin_other = (cin_s, cin_d) if forward else (cin_d, cin_s)

            def make(late, value):
                if part:
                    return value + (cin_other[s] if late else weight * other[s])
                if late:
                    value = value + weight * cin_mine[s]
                return th * value + mine[s]

            ends = (z == 0, z == RING - 1) if forward else (z == RING - 1, z == 0)
            copy, recv, send = (copy_p, recv_p, send_p) if forward else (copy_m, recv_m, send_m)
            chain(part, s, *ends, copy, recv, send, make)

        at(tau - from_left, 0, SLICES, lambda s: run(True, 0, s))
        at(tau - from_right, 0, SLICES, lambda s: run(False, 0, s))

        @pl.when(tau == need)
        def _():
            make_weights()

        at(tau - from_left, 0, SLICES, lambda s: run(True, 1, s))
        at(tau - from_right, 0, SLICES, lambda s: run(False, 1, s))

        def early_s(s):
            pass_s(s, lambda s: weights(s)[2] * l_ref[s])

        def early_d(s):
            pass_d(s, lambda s: weights(s)[1] * ld_ref[s])

        at(tau + LATE - DELAY - LAG * hops_s, LATE, SLICES, early_s)
        at(tau + LATE - DELAY - LAG * hops_d, LATE, SLICES, early_d)

        def late_s(s):
            pass_s(s, lambda s: weights(s)[2] * send_p[0, s] + recv_m[1, s])
            keep(s, recv_p[0, s] + weights(s)[1] * cin_s[s], cin_s, sp_ref)

        def late_d(s):
            pass_d(s, lambda s: weights(s)[1] * send_m[0, s] + recv_p[1, s])
            keep(s, recv_m[0, s] + weights(s)[2] * cin_d[s], cin_d, dp_ref)

        at(tau - far - LAG * hops_s, 0, LATE, late_s)
        at(tau - far - LAG * hops_d, 0, LATE, late_d)

        def whole(s):
            _, ahead, behind, _ = weights(s)
            state = recv_p[0, s] + ahead * (cin_s[s] + recv_m[1, s])
            state_d = recv_m[0, s] + behind * (cin_d[s] + recv_p[1, s])
            keep(s, state, cin_s, sp_ref)
            keep(s, state_d, cin_d, dp_ref)

        at(tau - far, LATE, SLICES, whole)

        @pl.when(tau == 0)
        def _():
            make_scores()

        beat = PER // 2
        place = over(tau, beat) + READY

        @pl.when((left_over(tau, beat) == 0) & (place < GROUPS))
        def _():
            prepare(choose(place))

        turn = left_over(tau, PER)

        @pl.when((tau >= PER) & (tau < SLICES + PER) & (left_over(turn, PIECES // 2) == 0))
        def _():
            local_work(over(tau, PER) - 1, over(turn, PIECES // 2))

        def both(c, _):
            done = jnp.where(c == 0, tau - far - LAG * jnp.maximum(hops_s, hops_d), tau - far)
            done = done - (PER - 1)
            low = jnp.where(c == 0, 0, LATE)
            high = jnp.where(c == 0, LATE, SLICES)

            @pl.when((done >= low) & (done < high) & (left_over(done, PER) == 0))
            def _():
                grads(over(done, PER))

            return 0

        lax.fori_loop(0, 2, both, 0)
        return 0

    lax.fori_loop(0, SLOTS, slot_body, 0)

    d_scores = jnp.where(mask_ref[...] > 0.5, ds_ref[...], 0.0)
    bq, cq = b_ref[...], c_ref[...]
    sh, sl = split2(d_scores)
    quarter = TOK // HEADS_AX

    def copy_rs(n, d):
        target = lax.rem(head + d, HEADS_AX)
        rows_of = pl.ds(pl.multiple_of(target * quarter, quarter), quarter)
        return remote(
            part_ref.at[n, rows_of],
            rs_ref.at[n, d],
            rs_send.at[n, d],
            rs_recv.at[n, d],
            {"head": target},
        )

    def copy_ag(n, d, slot):
        return remote(
            sum_ref.at[n],
            full_ref.at[n, slot],
            ag_send.at[n, d],
            ag_recv.at[n, d],
            {"head": lax.rem(head + d, HEADS_AX)},
        )

    part_ref[1] = enter * acc_ref[:, STATE:] + nn(sh, bq) + nn(sl, bq)
    for d in range(1, HEADS_AX):
        copy_rs(1, d).start()
    th, tl = split2(d_scores.T)
    part_ref[0] = leave * acc_ref[:, :STATE] + nn(th, cq) + nn(tl, cq)
    for d in range(1, HEADS_AX):
        copy_rs(0, d).start()

    tri = jnp.where(iota((TOK, TOK), 0) >= iota((TOK, TOK), 1), 1.0, 0.0).astype(BF16)
    dl = sum(nn(part[:HEADS], tri) for part in split3(rc_ref[...].T))
    gs_ref[...] = -(rate_col * dl)
    rate_part = -jnp.sum(step * dl, axis=1, keepdims=True)
    skip_part = sum(nt(ob_ref[...], part) for part in split3(sk_ref[...]))[:, :1]
    diag = iota((HEADS, 128), 0) == iota((HEADS, 128), 1)
    rate_row = jnp.sum(jnp.where(diag, rate_part, 0.0), axis=0, keepdims=True)
    skip_row = jnp.sum(jnp.where(diag, skip_part, 0.0), axis=0, keepdims=True)
    first = iota((8, 128), 0)
    vec_ref[...] = jnp.where(first == 0, rate_row, jnp.where(first == 1, skip_row, 0.0))

    swap = remote(vec_ref, vdp_ref, v_send.at[0], v_recv.at[0], {"dp": 1 - core})
    swap.start()
    swap.wait()
    vec2_ref[...] = vec_ref[...] + vdp_ref[...]
    vz_ref[z] = vec2_ref[...]

    def copy_z(d, slot):
        target = y * RING + lax.rem(z + d, RING)
        return remote(vec2_ref, vz_ref.at[slot], v_send.at[d], v_recv.at[d], {"seq": target})

    for d in range(1, RING):
        copy_z(d, z).start()
    mine_rows = pl.ds(pl.multiple_of(head * quarter, quarter), quarter)
    def drain(s, _):
        @pl.when(z < RING - 1)
        def _():
            copy_p(0, s).wait_send()
            copy_p(1, s).wait_send()

        @pl.when(z > 0)
        def _():
            copy_m(0, s).wait_send()
            copy_m(1, s).wait_send()

        @pl.when(y < ROWS - 1)
        def _():
            copy_s(s).wait_send()

        @pl.when(y > 0)
        def _():
            copy_d(s).wait_send()

        return 0

    lax.fori_loop(0, SLICES, drain, 0)

    for n in (1, 0):
        for d in range(1, HEADS_AX):
            copy_rs(n, d).wait()
        sum_ref[n] = part_ref[n, mine_rows] + rs_ref[n, 1] + rs_ref[n, 2] + rs_ref[n, 3]
        full_ref[n, head] = sum_ref[n]
        for d in range(1, HEADS_AX):
            copy_ag(n, d, head).start()

    for d in range(1, RING):
        copy_z(d, lax.rem(z + RING - d, RING)).wait()
    vec3_ref[...] = sum(vz_ref[n] for n in range(RING))
    vy_ref[y] = vec3_ref[...]

    def copy_y(d, slot):
        target = lax.rem(y + d, ROWS) * RING + z
        n = RING + d
        return remote(vec3_ref, vy_ref.at[slot], v_send.at[n], v_recv.at[n], {"seq": target})

    for d in range(1, ROWS):
        copy_y(d, y).start()
    for n, out_ref in ((1, gc_ref), (0, gb_ref)):
        for d in range(1, HEADS_AX):
            copy_ag(n, d, lax.rem(head + HEADS_AX - d, HEADS_AX)).wait()
        for m in range(HEADS_AX):
            out_ref[m * quarter : (m + 1) * quarter] = full_ref[n, m]
    for d in range(1, ROWS):
        copy_y(d, lax.rem(y + ROWS - d, ROWS)).wait()
    whole_vec = sum(vy_ref[n] for n in range(ROWS))
    gr_ref[...] = whole_vec[0:1, :HEADS]
    gk_ref[...] = whole_vec[1:2, :HEADS]


def hand_out(*refs):
    ins, outs, held, sems_in, sems_out = refs[:6], refs[6:12], refs[12:18], refs[18], refs[19]
    pieces = [(n, None) for n in range(1, 6)]
    pieces = [(0, pl.ds(m * TOK // 4, TOK // 4)) for m in range(4)] + pieces

    def cut(ref, rows):
        return ref if rows is None else ref.at[rows]

    loads, stores = [], []
    for m, (n, rows) in enumerate(pieces):
        there, here, out = cut(ins[n], rows), cut(held[n], rows), cut(outs[n], rows)
        loads.append(pltpu.make_async_copy(there, here, sems_in.at[m]))
        stores.append(pltpu.make_async_copy(here, out, sems_out.at[m]))
    for load in loads:
        load.start()
    for load, store in zip(loads, stores):
        load.wait()
        store.start()
    for store in stores:
        store.wait()


def on_device(inputs, proj_b, proj_c, step_size, decay_rate, skip_gain, doc_lengths, grad_out):
    vmem = pl.BlockSpec(memory_space=pltpu.VMEM)
    state = pltpu.VMEM((SLICES, HALF, 128), F32)
    message = pltpu.VMEM((2, SLICES, HALF, 128), F32)
    pair = pltpu.VMEM((2, SLICES, HALF, 128), BF16)
    sems = pltpu.SemaphoreType.DMA((SLICES,))
    both = pltpu.SemaphoreType.DMA((2, SLICES))
    tile = pltpu.VMEM((8, 128), F32)
    quarter = TOK // HEADS_AX
    scratch = [
        pltpu.VMEM((TOK, FEAT), BF16),
        pltpu.VMEM((TOK, FEAT), BF16),
        pltpu.VMEM((TOK, FEAT), BF16),
        pltpu.VMEM((TOK, FEAT), BF16),
        pltpu.VMEM((TOK, FEAT), BF16),
        pltpu.VMEM((TOK, FEAT), BF16),
        pltpu.VMEM((TOK, FEAT), F32),
        pltpu.VMEM((TOK, FEAT), F32),
        pltpu.VMEM((TOK, WIDE), F32),
        pltpu.VMEM((HEADS, FEAT), BF16),
        pltpu.VMEM((3, TOK, HEADS), BF16),
        pltpu.VMEM((2, TOK, TOK), BF16),
        pltpu.VMEM((2, TOK, TOK), BF16),
        pltpu.VMEM((TOK, TOK), F32),
        pltpu.VMEM((2, TOK, STATE), BF16),
        pltpu.VMEM((2, STATE, TOK), BF16),
        pltpu.VMEM((FEAT // 128, 8, 128), F32),
        pltpu.VMEM((FEAT // 128, 8, 128), F32),
        pltpu.VMEM((FEAT // 128, 8, 128), F32),
        pltpu.VMEM((RING, 8, 128), F32),
        pltpu.VMEM((TOK, TOK), F32),
        pltpu.VMEM((1, FEAT), F32),
        pltpu.VMEM((8, FEAT), F32),
        pltpu.VMEM((TOK, 128), F32),
        state,
        state,
        message,
        message,
        message,
        message,
        state,
        state,
        state,
        state,
        pair,
        pair,
        pltpu.VMEM((TOK, 2 * STATE), F32),
        pltpu.VMEM((2, TOK, STATE), F32),
        pltpu.VMEM((2, HEADS_AX, quarter, STATE), F32),
        pltpu.VMEM((2, quarter, STATE), F32),
        pltpu.VMEM((2, HEADS_AX, quarter, STATE), F32),
        tile,
        tile,
        tile,
        pltpu.VMEM((RING, 8, 128), F32),
        tile,
        pltpu.VMEM((ROWS, 8, 128), F32),
        both,
        both,
        both,
        both,
        sems,
        sems,
        sems,
        sems,
        pltpu.SemaphoreType.DMA((2, HEADS_AX)),
        pltpu.SemaphoreType.DMA((2, HEADS_AX)),
        pltpu.SemaphoreType.DMA((2, HEADS_AX)),
        pltpu.SemaphoreType.DMA((2, HEADS_AX)),
        pltpu.SemaphoreType.DMA((RING + ROWS,)),
        pltpu.SemaphoreType.DMA((RING + ROWS,)),
        pltpu.SemaphoreType.DMA((RING,)),
        pltpu.SemaphoreType.DMA((RING,)),
        pltpu.SemaphoreType.DMA((2,)),
    ]
    shapes = (
        jax.ShapeDtypeStruct((TOK, FEAT), BF16),
        jax.ShapeDtypeStruct((TOK, STATE), F32),
        jax.ShapeDtypeStruct((TOK, STATE), F32),
        jax.ShapeDtypeStruct((HEADS, TOK), F32),
        jax.ShapeDtypeStruct((1, HEADS), F32),
        jax.ShapeDtypeStruct((1, HEADS), F32),
    )
    anywhere = pl.BlockSpec(memory_space=pl.ANY)
    results = pl.pallas_call(
        kernel,
        out_shape=shapes,
        in_specs=[anywhere] * 2 + [vmem] * 6,
        out_specs=(vmem,) * 6,
        scratch_shapes=scratch,
        compiler_params=pltpu.CompilerParams(
            collective_id=0, has_side_effects=True, vmem_limit_bytes=56 << 20
        ),
    )(
        inputs[0],
        grad_out[0],
        proj_b[0],
        proj_c[0],
        step_size[0],
        decay_rate[None],
        skip_gain[None],
        doc_lengths,
    )
    grad_x, grad_b, grad_c, grad_step, grad_rate, grad_skip = pl.pallas_call(
        hand_out,
        out_shape=shapes,
        in_specs=[anywhere] * 6,
        out_specs=(anywhere,) * 6,
        scratch_shapes=[pltpu.VMEM(shape.shape, shape.dtype) for shape in shapes]
        + [pltpu.SemaphoreType.DMA((9,)), pltpu.SemaphoreType.DMA((9,))],
        compiler_params=pltpu.CompilerParams(vmem_limit_bytes=56 << 20),
    )(*results)
    return (
        grad_x[None],
        grad_b[None],
        grad_c[None],
        grad_step[None],
        grad_rate[0],
        grad_skip[0],
    )


def solution(mesh):
    in_specs = (
        P("dp", "seq", "head"),
        P("dp", "seq", None),
        P("dp", "seq", None),
        P("dp", "head", "seq"),
        P("head"),
        P("head"),
        P("dp", None),
        P("dp", "seq", "head"),
    )
    out_specs = (
        P("dp", "seq", "head"),
        P("dp", "seq", None),
        P("dp", "seq", None),
        P("dp", "head", "seq"),
        P("head"),
        P("head"),
    )
    return jax.shard_map(
        on_device, mesh=mesh, in_specs=in_specs, out_specs=out_specs, check_vma=False
    )
```

```python
import jax
import jax.numpy as jnp
from jax import lax
from jax.experimental import pallas as pl
from jax.experimental.pallas import tpu as pltpu
from jax.sharding import PartitionSpec as P

F32 = jnp.float32
BF16 = jnp.bfloat16
MESH = pl.DeviceIdType.MESH

ROWS = 4
RING = 8
SEQ = ROWS * RING
HEADS_AX = 4
TOK = 256
HEADS = 32
HEAD_DIM = 64
STATE = 128
FEAT = HEADS * HEAD_DIM
WIDE = 256
GROUPS = FEAT // WIDE
PIECES = 2
PER = 2 * PIECES
SLICES = PER * GROUPS
HALF = STATE // PIECES
LATE = SLICES // 2
HOP = 11 * PIECES // 2
LAG = 3 * PIECES // 2
DELAY = PER + 2
SLOTS = HOP * (RING - 1) // 4 + SLICES
ORDER = (0, 1, 4, 2, 5, 3, 6, 7)
READY = 1


def nn(a, b):
    return lax.dot_general(a, b, (((1,), (0,)), ((), ())), preferred_element_type=F32)


def nt(a, b):
    return lax.dot_general(a, b, (((1,), (1,)), ((), ())), preferred_element_type=F32)


def split2(value):
    high = value.astype(BF16)
    return high, (value - high.astype(F32)).astype(BF16)


def split3(value):
    high = value.astype(BF16)
    rest = value - high.astype(F32)
    middle = rest.astype(BF16)
    return high, middle, (rest - middle.astype(F32)).astype(BF16)


def over(n, size):
    return lax.shift_right_arithmetic(n, jnp.int32(size.bit_length() - 1))


def left_over(n, size):
    return lax.bitwise_and(n, jnp.int32(size - 1))


def iota(shape, dim):
    return lax.broadcasted_iota(jnp.int32, shape, dim)


def kernel(
    x_hbm,
    dy_hbm,
    b_ref,
    c_ref,
    step_ref,
    rate_ref,
    skip_ref,
    len_ref,
    gx_ref,
    gb_ref,
    gc_ref,
    gs_ref,
    gr_ref,
    gk_ref,
    x_ref,
    dy_ref,
    xh_ref,
    xl_ref,
    dyh_ref,
    dyl_ref,
    em_ref,
    dx_ref,
    yl_ref,
    ob_ref,
    rt_ref,
    sm_ref,
    smt_ref,
    ds_ref,
    cb_ref,
    cbt_ref,
    g_ref,
    th_ref,
    w_ref,
    thz_ref,
    mask_ref,
    skr_ref,
    skx_ref,
    sk_ref,
    rc_ref,
    l_ref,
    ld_ref,
    recv_p,
    recv_m,
    send_p,
    send_m,
    cin_s,
    cin_d,
    ysend_s,
    ysend_d,
    sp_ref,
    dp_ref,
    acc_ref,
    part_ref,
    rs_ref,
    sum_ref,
    full_ref,
    vec_ref,
    vdp_ref,
    vec2_ref,
    vz_ref,
    vec3_ref,
    vy_ref,
    p_send,
    p_recv,
    m_send,
    m_recv,
    s_send,
    s_recv,
    d_send,
    d_recv,
    rs_send,
    rs_recv,
    ag_send,
    ag_recv,
    v_send,
    v_recv,
    t_send,
    t_recv,
    in_sems,
):
    core = lax.axis_index("dp")
    k = lax.axis_index("seq")
    head = lax.axis_index("head")
    y = over(k, RING)
    z = left_over(k, RING)
    right = lax.rem(k + 1, SEQ)
    left = lax.rem(k + SEQ - 1, SEQ)
    up = lax.rem(k + RING, SEQ)
    down = lax.rem(k + SEQ - RING, SEQ)

    peers = [{"dp": 1 - core}]
    peers += [{"seq": y * RING + lax.rem(z + d, RING)} for d in range(1, RING)]
    peers += [{"seq": lax.rem(y + d, ROWS) * RING + z} for d in range(1, ROWS)]
    peers += [{"head": lax.rem(head + d, HEADS_AX)} for d in range(1, HEADS_AX)]
    barrier = pltpu.get_barrier_semaphore()
    for peer in peers:
        pl.semaphore_signal(barrier, inc=1, device_id=peer, device_id_type=MESH)

    load_x = pltpu.make_async_copy(x_hbm, x_ref, in_sems.at[0])
    load_dy = pltpu.make_async_copy(dy_hbm, dy_ref, in_sems.at[1])
    load_x.start()
    load_dy.start()

    lens = len_ref[...].astype(F32)
    docs = lens.shape[1]
    sub, lane = iota((docs, docs), 0), iota((docs, docs), 1)
    lens_col = jnp.sum(jnp.where(sub == lane, lens, 0.0), axis=1, keepdims=True)
    ends_row = jnp.sum(jnp.where(sub <= lane, lens_col, 0.0), axis=0, keepdims=True)
    ends_col = jnp.sum(jnp.where(lane <= sub, lens, 0.0), axis=1, keepdims=True)
    anchor = k * TOK
    pos_c = (anchor + iota((TOK, docs), 0)).astype(F32)
    pos_r = (anchor + iota((docs, TOK), 1)).astype(F32)
    one_r = (anchor + iota((1, docs), 0)).astype(F32)
    doc_c = jnp.sum(jnp.where(ends_row <= pos_c, 1.0, 0.0), axis=1, keepdims=True)
    doc_r = jnp.sum(jnp.where(ends_col <= pos_r, 1.0, 0.0), axis=0, keepdims=True)
    before = jnp.sum(jnp.where(ends_row <= one_r - 1.0, 1.0, 0.0), axis=1, keepdims=True)
    before = jnp.where(one_r[:, :1] < 0.5, -1.0, before)
    last = jnp.sum(jnp.where(ends_row <= one_r + (TOK - 1.0), 1.0, 0.0), axis=1, keepdims=True)
    enter = jnp.where(doc_c == before, 1.0, 0.0)
    leave = jnp.where(doc_c == last, 1.0, 0.0)
    same_end = jnp.where(last == before, 1.0, 0.0)

    bq, cq = b_ref[...], c_ref[...]
    rows, cols = iota((TOK, TOK), 0), iota((TOK, TOK), 1)
    cm, bm = cq.astype(F32) * enter, bq.astype(F32) * leave
    cb_ref[0], cb_ref[1] = cm.astype(BF16), bm.astype(BF16)
    cbt_ref[0], cbt_ref[1] = cm.T.astype(BF16), bm.T.astype(BF16)

    hsub, hlane = iota((HEADS, HEADS), 0), iota((HEADS, HEADS), 1)
    rate_col = jnp.sum(jnp.where(hsub == hlane, rate_ref[...], 0.0), axis=1, keepdims=True)
    skip_col = jnp.sum(jnp.where(hsub == hlane, skip_ref[...], 0.0), axis=1, keepdims=True)
    step = step_ref[...]
    tri = jnp.where(rows >= cols, 1.0, 0.0).astype(BF16)
    owner = jnp.where(over(iota((HEADS, FEAT), 1), HEAD_DIM) == iota((HEADS, FEAT), 0), 1.0, 0.0)
    ob_ref[...] = owner.astype(BF16)
    skx_ref[...] = jnp.sum(owner * skip_col, axis=0, keepdims=True)
    running = sum(nt(tri, part) for part in split3(-(step * rate_col)))
    rt_ref[0], rt_ref[1], rt_ref[2] = split3(running)

    def remote(src, dst, send, recv, device):
        return pltpu.make_async_remote_copy(
            src_ref=src,
            dst_ref=dst,
            send_sem=send,
            recv_sem=recv,
            device_id=device,
            device_id_type=MESH,
        )

    passing = jnp.exp(running[TOK - 1 :, :]) * same_end
    wide = jnp.concatenate([passing, jnp.zeros((1, 128 - HEADS), F32)], axis=1)
    thz_ref[z] = jnp.broadcast_to(wide, (8, 128))

    def copy_t(d, slot):
        target = y * RING + lax.rem(z + d, RING)
        return remote(
            thz_ref.at[z], thz_ref.at[slot], t_send.at[d], t_recv.at[d], {"seq": target}
        )

    def prepare(i):
        at = pl.ds(pl.multiple_of(i * WIDE, WIDE), WIDE)
        ob = ob_ref[:, at]
        rx = nn(rt_ref[0], ob) + nn(rt_ref[1], ob) + nn(rt_ref[2], ob)
        end = rx[TOK - 1 : TOK, :]
        mid = 0.5 * end
        em = jnp.exp(mid - rx)
        em_ref[:, at] = em
        x_f, dy_f = x_ref[:, at].astype(F32), dy_ref[:, at].astype(F32)
        sk_ref[:, at] = jnp.broadcast_to(jnp.sum(x_f * dy_f, axis=0, keepdims=True), (8, WIDE))
        xh, xl = split2(em * x_f)
        dyh, dyl = split2(jnp.exp(rx - mid) * dy_f)
        xh_ref[:, at], xl_ref[:, at], dyh_ref[:, at], dyl_ref[:, at] = xh, xl, dyh, dyl
        g = jnp.exp(mid)
        th = jnp.exp(end) * same_end
        local = g * (nn(cbt_ref[1], xh) + nn(cbt_ref[1], xl))
        local_d = g * (nn(cbt_ref[0], dyh) + nn(cbt_ref[0], dyl))
        for q in range(2):
            cut = slice(q * 128, q * 128 + 128)
            g_ref[2 * i + q] = jnp.broadcast_to(g[:, cut], (8, 128))
            th_ref[2 * i + q] = jnp.broadcast_to(th[:, cut], (8, 128))
            for n in range(PIECES):
                some = slice(n * HALF, n * HALF + HALF)
                l_ref[PER * i + PIECES * q + n] = local[some, cut]
                ld_ref[PER * i + PIECES * q + n] = local_d[some, cut]

    def choose(place):
        chosen = 0
        for n in range(1, GROUPS):
            chosen = jnp.where(place == n, ORDER[n], chosen)
        return chosen

    def prepare_next(place, _):
        prepare(choose(place))
        return 0

    load_x.wait()
    load_dy.wait()
    lax.fori_loop(0, READY, prepare_next, 0)
    pl.semaphore_wait(barrier, len(peers))
    for d in range(1, RING):
        copy_t(d, z).start()

    def make_weights():
        for d in range(1, RING):
            copy_t(d, lax.rem(z + RING - d, RING)).wait()
        ones = jnp.ones((8, 128), F32)
        ahead, behind = ones, ones
        for n in range(RING):
            ahead = ahead * jnp.where(n < z, thz_ref[n], ones)
            behind = behind * jnp.where(n > z, thz_ref[n], ones)
        pick = iota((8, 128), 0)
        row = ahead * behind * thz_ref[z]
        table = jnp.where(pick == 0, ahead, jnp.where(pick == 1, behind, row))
        table = sum(nn(part[:, :HEADS], ob_ref[...]) for part in split3(table))
        for n in range(FEAT // 128):
            w_ref[n] = table[:, n * 128 : (n + 1) * 128]

    def make_scores():
        same = doc_c == doc_r
        lower = same & (iota((TOK, TOK), 0) >= iota((TOK, TOK), 1))
        upper = same & (iota((TOK, TOK), 0) <= iota((TOK, TOK), 1))
        sm_ref[0], sm_ref[1] = split2(jnp.where(lower, nt(c_ref[...], b_ref[...]), 0.0))
        smt_ref[0], smt_ref[1] = split2(jnp.where(upper, nt(b_ref[...], c_ref[...]), 0.0))
        mask_ref[...] = jnp.where(lower, 1.0, 0.0)

    w_ref[...] = jnp.ones_like(w_ref)
    acc_ref[...] = jnp.zeros_like(acc_ref)
    rc_ref[...] = jnp.zeros_like(rc_ref)
    ds_ref[...] = jnp.zeros_like(ds_ref)

    def copy_p(part, s):
        return remote(
            send_p.at[part, s],
            recv_p.at[part, s],
            p_send.at[part, s],
            p_recv.at[part, s],
            {"seq": right},
        )

    def copy_m(part, s):
        return remote(
            send_m.at[part, s],
            recv_m.at[part, s],
            m_send.at[part, s],
            m_recv.at[part, s],
            {"seq": left},
        )

    def copy_s(s):
        return remote(ysend_s.at[s], cin_s.at[s], s_send.at[s], s_recv.at[s], {"seq": up})

    def copy_d(s):
        return remote(ysend_d.at[s], cin_d.at[s], d_send.at[s], d_recv.at[s], {"seq": down})

    def weights(s):
        fb = over(s, PIECES)
        return th_ref[fb, 0:1], w_ref[fb, 0:1], w_ref[fb, 1:2], w_ref[fb, 2:3]

    def chain(part, s, first, final, copy, recv, send, make):
        @pl.when(first)
        def _():
            recv[part, s] = jnp.zeros((HALF, 128), F32)

        @pl.when(jnp.logical_not(first))
        def _():
            copy(part, s).wait_recv()

        for late in range(2):

            @pl.when(s >= LATE if late else s < LATE)
            def _():
                send[part, s] = make(late, recv[part, s])

        @pl.when(jnp.logical_not(final))
        def _():
            copy(part, s).start()

    def pass_on(s, has_recv, has_send, copy, cin, ysend, total):
        @pl.when(has_recv)
        def _():
            copy(s).wait_recv()

        @pl.when(jnp.logical_not(has_recv))
        def _():
            cin[s] = jnp.zeros((HALF, 128), F32)

        @pl.when(has_send)
        def _():
            ysend[s] = total(s) + weights(s)[3] * cin[s]
            copy(s).start()

    def pass_s(s, total):
        pass_on(s, y > 0, y < ROWS - 1, copy_s, cin_s, ysend_s, total)

    def pass_d(s, total):
        pass_on(s, y < ROWS - 1, y > 0, copy_d, cin_d, ysend_d, total)

    def keep(s, state, cin, dest):
        cin[s] = state
        dest[0, s], dest[1, s] = split2(state * g_ref[over(s, PIECES), 0:1])

    def own_heads(i):
        shape = (WIDE, 128)
        hit = over(iota(shape, 0), HEAD_DIM) + 4 * i == iota(shape, 1)
        return jnp.where(hit, 1.0, 0.0).astype(BF16)

    def add_products(i, at, y_part, dx_part, extra):
        dyp = dyh_ref[:, at].astype(F32) + dyl_ref[:, at].astype(F32)
        xp = xh_ref[:, at].astype(F32) + xl_ref[:, at].astype(F32)
        prod = dyp * y_part - xp * dx_part
        if extra is not None:
            prod = prod + jnp.where(iota((TOK, WIDE), 0) == TOK - 1, extra, 0.0)
        heads = own_heads(i)
        rc_ref[...] += sum(nn(part, heads) for part in split3(prod))

    def local_work(i, turn):
        at = pl.ds(pl.multiple_of(i * WIDE, WIDE), WIDE)

        @pl.when(turn == 0)
        def _():
            yl_ref[...] = (
                nn(sm_ref[0], xh_ref[:, at])
                + nn(sm_ref[0], xl_ref[:, at])
                + nn(sm_ref[1], xh_ref[:, at])
            )

        @pl.when(turn == 1)
        def _():
            dx_ref[:, at] = (
                nn(smt_ref[0], dyh_ref[:, at])
                + nn(smt_ref[0], dyl_ref[:, at])
                + nn(smt_ref[1], dyh_ref[:, at])
            )

        @pl.when(turn == 2)
        def _():
            add_products(i, at, yl_ref[...], dx_ref[:, at], None)

        @pl.when(turn == 3)
        def _():
            ds_ref[...] += (
                nt(dyh_ref[:, at], xh_ref[:, at])
                + nt(dyh_ref[:, at], xl_ref[:, at])
                + nt(dyl_ref[:, at], xh_ref[:, at])
            )

    def states(ref, part, i):
        def column(q):
            some = [ref[part, PER * i + PIECES * q + n] for n in range(PIECES)]
            return jnp.concatenate(some, axis=0)

        return jnp.concatenate([column(0), column(1)], axis=1)

    def grads(i):
        at = pl.ds(pl.multiple_of(i * WIDE, WIDE), WIDE)
        sh, sl = states(sp_ref, 0, i), states(sp_ref, 1, i)
        dh, dl = states(dp_ref, 0, i), states(dp_ref, 1, i)
        xh, xl, dyh, dyl = xh_ref[:, at], xl_ref[:, at], dyh_ref[:, at], dyl_ref[:, at]
        acc_ref[:, :STATE] += nt(xh, dh) + nt(xl, dh) + nt(xh, dl)
        acc_ref[:, STATE:] += nt(dyh, sh) + nt(dyl, sh) + nt(dyh, sl)
        y_part = nn(cb_ref[0], sh) + nn(cb_ref[0], sl)
        dx_part = nn(cb_ref[1], dh) + nn(cb_ref[1], dl)
        ends = []
        for q in range(2):
            total = 0.0
            for n in range(PIECES):
                s = PER * i + PIECES * q + n
                out = th_ref[2 * i + q, 0:1] * cin_s[s] + l_ref[s]
                total = total + jnp.sum(out * cin_d[s], axis=0, keepdims=True)
            ends.append(total)
        add_products(i, at, y_part, dx_part, jnp.concatenate(ends, axis=1))
        whole = em_ref[:, at] * (dx_ref[:, at] + dx_part)
        whole = whole + skx_ref[:, at] * dy_ref[:, at].astype(F32)
        gx_ref[:, at] = whole.astype(BF16)

    from_left = over(HOP * z, 4)
    from_right = over(HOP * (RING - 1 - z), 4)
    far = jnp.maximum(from_left, from_right)
    need = jnp.where((z == 0) | (z == RING - 1), DELAY, over(HOP, 4))
    hops_s, hops_d = y, ROWS - 1 - y

    def slot_body(tau, _):
        def at(n, low, high, work):
            @pl.when((n >= low) & (n < high))
            def _():
                work(n)

        def run(forward, part, s):
            th, ahead, behind, _ = weights(s)
            weight = ahead if forward else behind
            mine, other = (l_ref, ld_ref) if forward else (ld_ref, l_ref)
            cin_mine, cin_other = (cin_s, cin_d) if forward else (cin_d, cin_s)

            def make(late, value):
                if part:
                    return value + (cin_other[s] if late else weight * other[s])
                if late:
                    value = value + weight * cin_mine[s]
                return th * value + mine[s]

            ends = (z == 0, z == RING - 1) if forward else (z == RING - 1, z == 0)
            copy, recv, send = (copy_p, recv_p, send_p) if forward else (copy_m, recv_m, send_m)
            chain(part, s, *ends, copy, recv, send, make)

        at(tau - from_left, 0, SLICES, lambda s: run(True, 0, s))
        at(tau - from_right, 0, SLICES, lambda s: run(False, 0, s))

        @pl.when(tau == need)
        def _():
            make_weights()

        at(tau - from_left, 0, SLICES, lambda s: run(True, 1, s))
        at(tau - from_right, 0, SLICES, lambda s: run(False, 1, s))

        def early_s(s):
            pass_s(s, lambda s: weights(s)[2] * l_ref[s])

        def early_d(s):
            pass_d(s, lambda s: weights(s)[1] * ld_ref[s])

        at(tau + LATE - DELAY - LAG * hops_s, LATE, SLICES, early_s)
        at(tau + LATE - DELAY - LAG * hops_d, LATE, SLICES, early_d)

        def late_s(s):
            pass_s(s, lambda s: weights(s)[2] * send_p[0, s] + recv_m[1, s])
            keep(s, recv_p[0, s] + weights(s)[1] * cin_s[s], cin_s, sp_ref)

        def late_d(s):
            pass_d(s, lambda s: weights(s)[1] * send_m[0, s] + recv_p[1, s])
            keep(s, recv_m[0, s] + weights(s)[2] * cin_d[s], cin_d, dp_ref)

        at(tau - far - LAG * hops_s, 0, LATE, late_s)
        at(tau - far - LAG * hops_d, 0, LATE, late_d)

        def whole(s):
            _, ahead, behind, _ = weights(s)
            state = recv_p[0, s] + ahead * (cin_s[s] + recv_m[1, s])
            state_d = recv_m[0, s] + behind * (cin_d[s] + recv_p[1, s])
            keep(s, state, cin_s, sp_ref)
            keep(s, state_d, cin_d, dp_ref)

        at(tau - far, LATE, SLICES, whole)

        @pl.when(tau == 1)
        def _():
            make_scores()

        beat = PER // 2
        place = over(tau, beat) + READY

        @pl.when((left_over(tau, beat) == 0) & (place < GROUPS))
        def _():
            prepare(choose(place))

        @pl.when(tau == SLICES + PER)
        def _():
            d_scores = jnp.where(mask_ref[...] > 0.5, ds_ref[...], 0.0)
            sh, sl = split2(d_scores)
            part_ref[1] = nn(sh, b_ref[...]) + nn(sl, b_ref[...])
            th, tl = split2(d_scores.T)
            part_ref[0] = nn(th, c_ref[...]) + nn(tl, c_ref[...])

        @pl.when(tau == SLICES + PER + 1)
        def _():
            skip_part = sum(nt(ob_ref[...], part) for part in split3(sk_ref[...]))[:, :1]
            diag = iota((HEADS, 128), 0) == iota((HEADS, 128), 1)
            skip_row = jnp.sum(jnp.where(diag, skip_part, 0.0), axis=0, keepdims=True)
            skr_ref[...] = jnp.broadcast_to(skip_row, (8, 128))

        turn = left_over(tau, PER)

        @pl.when((tau >= PER) & (tau < SLICES + PER) & (left_over(turn, PIECES // 2) == 0))
        def _():
            local_work(over(tau, PER) - 1, over(turn, PIECES // 2))

        def both(c, _):
            done = jnp.where(c == 0, tau - far - LAG * jnp.maximum(hops_s, hops_d), tau - far)
            done = done - (PER - 1)
            low = jnp.where(c == 0, 0, LATE)
            high = jnp.where(c == 0, LATE, SLICES)

            @pl.when((done >= low) & (done < high) & (left_over(done, PER) == 0))
            def _():
                grads(over(done, PER))

            return 0

        lax.fori_loop(0, 2, both, 0)
        return 0

    lax.fori_loop(0, SLOTS, slot_body, 0)

    quarter = TOK // HEADS_AX

    def copy_rs(n, d):
        target = lax.rem(head + d, HEADS_AX)
        rows_of = pl.ds(pl.multiple_of(target * quarter, quarter), quarter)
        return remote(
            part_ref.at[n, rows_of],
            rs_ref.at[n, d],
            rs_send.at[n, d],
            rs_recv.at[n, d],
            {"head": target},
        )

    def copy_ag(n, d, slot):
        return remote(
            sum_ref.at[n],
            full_ref.at[n, slot],
            ag_send.at[n, d],
            ag_recv.at[n, d],
            {"head": lax.rem(head + d, HEADS_AX)},
        )

    part_ref[1] += enter * acc_ref[:, STATE:]
    for d in range(1, HEADS_AX):
        copy_rs(1, d).start()
    part_ref[0] += leave * acc_ref[:, :STATE]
    for d in range(1, HEADS_AX):
        copy_rs(0, d).start()

    tri = jnp.where(iota((TOK, TOK), 0) >= iota((TOK, TOK), 1), 1.0, 0.0).astype(BF16)
    dl = sum(nn(part[:HEADS], tri) for part in split3(rc_ref[...].T))
    gs_ref[...] = -(rate_col * dl)
    rate_part = -jnp.sum(step * dl, axis=1, keepdims=True)
    diag = iota((HEADS, 128), 0) == iota((HEADS, 128), 1)
    rate_row = jnp.sum(jnp.where(diag, rate_part, 0.0), axis=0, keepdims=True)
    first = iota((8, 128), 0)
    vec_ref[...] = jnp.where(first == 0, rate_row, jnp.where(first == 1, skr_ref[...], 0.0))

    swap = remote(vec_ref, vdp_ref, v_send.at[0], v_recv.at[0], {"dp": 1 - core})
    swap.start()
    swap.wait()
    vec2_ref[...] = vec_ref[...] + vdp_ref[...]
    vz_ref[z] = vec2_ref[...]

    def copy_z(d, slot):
        target = y * RING + lax.rem(z + d, RING)
        return remote(vec2_ref, vz_ref.at[slot], v_send.at[d], v_recv.at[d], {"seq": target})

    for d in range(1, RING):
        copy_z(d, z).start()
    mine_rows = pl.ds(pl.multiple_of(head * quarter, quarter), quarter)
    def drain(s, _):
        @pl.when(z < RING - 1)
        def _():
            copy_p(0, s).wait_send()
            copy_p(1, s).wait_send()

        @pl.when(z > 0)
        def _():
            copy_m(0, s).wait_send()
            copy_m(1, s).wait_send()

        @pl.when(y < ROWS - 1)
        def _():
            copy_s(s).wait_send()

        @pl.when(y > 0)
        def _():
            copy_d(s).wait_send()

        return 0

    lax.fori_loop(0, SLICES, drain, 0)

    for n in (1, 0):
        for d in range(1, HEADS_AX):
            copy_rs(n, d).wait()
        sum_ref[n] = part_ref[n, mine_rows] + rs_ref[n, 1] + rs_ref[n, 2] + rs_ref[n, 3]
        full_ref[n, head] = sum_ref[n]
        for d in range(1, HEADS_AX):
            copy_ag(n, d, head).start()

    for d in range(1, RING):
        copy_z(d, lax.rem(z + RING - d, RING)).wait()
    vec3_ref[...] = sum(vz_ref[n] for n in range(RING))
    vy_ref[y] = vec3_ref[...]

    def copy_y(d, slot):
        target = lax.rem(y + d, ROWS) * RING + z
        n = RING + d
        return remote(vec3_ref, vy_ref.at[slot], v_send.at[n], v_recv.at[n], {"seq": target})

    for d in range(1, ROWS):
        copy_y(d, y).start()
    for n, out_ref in ((1, gc_ref), (0, gb_ref)):
        for d in range(1, HEADS_AX):
            copy_ag(n, d, lax.rem(head + HEADS_AX - d, HEADS_AX)).wait()
        for m in range(HEADS_AX):
            out_ref[m * quarter : (m + 1) * quarter] = full_ref[n, m]
    for d in range(1, ROWS):
        copy_y(d, lax.rem(y + ROWS - d, ROWS)).wait()
    whole_vec = sum(vy_ref[n] for n in range(ROWS))
    gr_ref[...] = whole_vec[0:1, :HEADS]
    gk_ref[...] = whole_vec[1:2, :HEADS]


def hand_out(*refs):
    ins, outs, held, sems_in, sems_out = refs[:6], refs[6:12], refs[12:18], refs[18], refs[19]
    pieces = [(n, None) for n in range(1, 6)]
    pieces = [(0, pl.ds(m * TOK // 4, TOK // 4)) for m in range(4)] + pieces

    def cut(ref, rows):
        return ref if rows is None else ref.at[rows]

    loads, stores = [], []
    for m, (n, rows) in enumerate(pieces):
        there, here, out = cut(ins[n], rows), cut(held[n], rows), cut(outs[n], rows)
        loads.append(pltpu.make_async_copy(there, here, sems_in.at[m]))
        stores.append(pltpu.make_async_copy(here, out, sems_out.at[m]))
    for load in loads:
        load.start()
    for load, store in zip(loads, stores):
        load.wait()
        store.start()
    for store in stores:
        store.wait()


def on_device(inputs, proj_b, proj_c, step_size, decay_rate, skip_gain, doc_lengths, grad_out):
    vmem = pl.BlockSpec(memory_space=pltpu.VMEM)
    state = pltpu.VMEM((SLICES, HALF, 128), F32)
    message = pltpu.VMEM((2, SLICES, HALF, 128), F32)
    pair = pltpu.VMEM((2, SLICES, HALF, 128), BF16)
    sems = pltpu.SemaphoreType.DMA((SLICES,))
    both = pltpu.SemaphoreType.DMA((2, SLICES))
    tile = pltpu.VMEM((8, 128), F32)
    quarter = TOK // HEADS_AX
    scratch = [
        pltpu.VMEM((TOK, FEAT), BF16),
        pltpu.VMEM((TOK, FEAT), BF16),
        pltpu.VMEM((TOK, FEAT), BF16),
        pltpu.VMEM((TOK, FEAT), BF16),
        pltpu.VMEM((TOK, FEAT), BF16),
        pltpu.VMEM((TOK, FEAT), BF16),
        pltpu.VMEM((TOK, FEAT), F32),
        pltpu.VMEM((TOK, FEAT), F32),
        pltpu.VMEM((TOK, WIDE), F32),
        pltpu.VMEM((HEADS, FEAT), BF16),
        pltpu.VMEM((3, TOK, HEADS), BF16),
        pltpu.VMEM((2, TOK, TOK), BF16),
        pltpu.VMEM((2, TOK, TOK), BF16),
        pltpu.VMEM((TOK, TOK), F32),
        pltpu.VMEM((2, TOK, STATE), BF16),
        pltpu.VMEM((2, STATE, TOK), BF16),
        pltpu.VMEM((FEAT // 128, 8, 128), F32),
        pltpu.VMEM((FEAT // 128, 8, 128), F32),
        pltpu.VMEM((FEAT // 128, 8, 128), F32),
        pltpu.VMEM((RING, 8, 128), F32),
        pltpu.VMEM((TOK, TOK), F32),
        tile,
        pltpu.VMEM((1, FEAT), F32),
        pltpu.VMEM((8, FEAT), F32),
        pltpu.VMEM((TOK, 128), F32),
        state,
        state,
        message,
        message,
        message,
        message,
        state,
        state,
        state,
        state,
        pair,
        pair,
        pltpu.VMEM((TOK, 2 * STATE), F32),
        pltpu.VMEM((2, TOK, STATE), F32),
        pltpu.VMEM((2, HEADS_AX, quarter, STATE), F32),
        pltpu.VMEM((2, quarter, STATE), F32),
        pltpu.VMEM((2, HEADS_AX, quarter, STATE), F32),
        tile,
        tile,
        tile,
        pltpu.VMEM((RING, 8, 128), F32),
        tile,
        pltpu.VMEM((ROWS, 8, 128), F32),
        both,
        both,
        both,
        both,
        sems,
        sems,
        sems,
        sems,
        pltpu.SemaphoreType.DMA((2, HEADS_AX)),
        pltpu.SemaphoreType.DMA((2, HEADS_AX)),
        pltpu.SemaphoreType.DMA((2, HEADS_AX)),
        pltpu.SemaphoreType.DMA((2, HEADS_AX)),
        pltpu.SemaphoreType.DMA((RING + ROWS,)),
        pltpu.SemaphoreType.DMA((RING + ROWS,)),
        pltpu.SemaphoreType.DMA((RING,)),
        pltpu.SemaphoreType.DMA((RING,)),
        pltpu.SemaphoreType.DMA((2,)),
    ]
    shapes = (
        jax.ShapeDtypeStruct((TOK, FEAT), BF16),
        jax.ShapeDtypeStruct((TOK, STATE), F32),
        jax.ShapeDtypeStruct((TOK, STATE), F32),
        jax.ShapeDtypeStruct((HEADS, TOK), F32),
        jax.ShapeDtypeStruct((1, HEADS), F32),
        jax.ShapeDtypeStruct((1, HEADS), F32),
    )
    anywhere = pl.BlockSpec(memory_space=pl.ANY)
    results = pl.pallas_call(
        kernel,
        out_shape=shapes,
        in_specs=[anywhere] * 2 + [vmem] * 6,
        out_specs=(vmem,) * 6,
        scratch_shapes=scratch,
        compiler_params=pltpu.CompilerParams(
            collective_id=0, has_side_effects=True, vmem_limit_bytes=56 << 20
        ),
    )(
        inputs[0],
        grad_out[0],
        proj_b[0],
        proj_c[0],
        step_size[0],
        decay_rate[None],
        skip_gain[None],
        doc_lengths,
    )
    grad_x, grad_b, grad_c, grad_step, grad_rate, grad_skip = pl.pallas_call(
        hand_out,
        out_shape=shapes,
        in_specs=[anywhere] * 6,
        out_specs=(anywhere,) * 6,
        scratch_shapes=[pltpu.VMEM(shape.shape, shape.dtype) for shape in shapes]
        + [pltpu.SemaphoreType.DMA((9,)), pltpu.SemaphoreType.DMA((9,))],
        compiler_params=pltpu.CompilerParams(vmem_limit_bytes=56 << 20),
    )(*results)
    return (
        grad_x[None],
        grad_b[None],
        grad_c[None],
        grad_step[None],
        grad_rate[0],
        grad_skip[0],
    )


def solution(mesh):
    in_specs = (
        P("dp", "seq", "head"),
        P("dp", "seq", None),
        P("dp", "seq", None),
        P("dp", "head", "seq"),
        P("head"),
        P("head"),
        P("dp", None),
        P("dp", "seq", "head"),
    )
    out_specs = (
        P("dp", "seq", "head"),
        P("dp", "seq", None),
        P("dp", "seq", None),
        P("dp", "head", "seq"),
        P("head"),
        P("head"),
    )
    return jax.shard_map(
        on_device, mesh=mesh, in_specs=in_specs, out_specs=out_specs, check_vma=False
    )
```

```python
import jax
import jax.numpy as jnp
from jax import lax
from jax.experimental import pallas as pl
from jax.experimental.pallas import tpu as pltpu
from jax.sharding import PartitionSpec as P

F32 = jnp.float32
BF16 = jnp.bfloat16
MESH = pl.DeviceIdType.MESH

ROWS = 4
RING = 8
SEQ = ROWS * RING
HEADS_AX = 4
TOK = 256
HEADS = 32
HEAD_DIM = 64
STATE = 128
FEAT = HEADS * HEAD_DIM
WIDE = 256
GROUPS = FEAT // WIDE
PIECES = 2
PER = 2 * PIECES
SLICES = PER * GROUPS
HALF = STATE // PIECES
LATE = SLICES // 2
HOP = 11 * PIECES // 2
LAG = 3 * PIECES // 2
DELAY = PER + 2
SLOTS = HOP * (RING - 1) // 4 + SLICES
ORDER = (0, 1, 4, 2, 5, 3, 6, 7)
READY = 1


def nn(a, b):
    return lax.dot_general(a, b, (((1,), (0,)), ((), ())), preferred_element_type=F32)


def nt(a, b):
    return lax.dot_general(a, b, (((1,), (1,)), ((), ())), preferred_element_type=F32)


def split2(value):
    high = value.astype(BF16)
    return high, (value - high.astype(F32)).astype(BF16)


def split3(value):
    high = value.astype(BF16)
    rest = value - high.astype(F32)
    middle = rest.astype(BF16)
    return high, middle, (rest - middle.astype(F32)).astype(BF16)


def over(n, size):
    return lax.shift_right_arithmetic(n, jnp.int32(size.bit_length() - 1))


def left_over(n, size):
    return lax.bitwise_and(n, jnp.int32(size - 1))


def iota(shape, dim):
    return lax.broadcasted_iota(jnp.int32, shape, dim)


def kernel(
    x_hbm,
    dy_hbm,
    b_ref,
    c_ref,
    step_ref,
    rate_ref,
    skip_ref,
    len_ref,
    gx_ref,
    gb_ref,
    gc_ref,
    gs_ref,
    gr_ref,
    gk_ref,
    x_ref,
    dy_ref,
    xh_ref,
    xl_ref,
    dyh_ref,
    dyl_ref,
    em_ref,
    dx_ref,
    yl_ref,
    ob_ref,
    rt_ref,
    sm_ref,
    smt_ref,
    ds_ref,
    cb_ref,
    cbt_ref,
    g_ref,
    th_ref,
    w_ref,
    thz_ref,
    mask_ref,
    skr_ref,
    skx_ref,
    sk_ref,
    rc_ref,
    l_ref,
    ld_ref,
    recv_p,
    recv_m,
    send_p,
    send_m,
    cin_s,
    cin_d,
    ysend_s,
    ysend_d,
    sp_ref,
    dp_ref,
    acc_ref,
    part_ref,
    rs_ref,
    sum_ref,
    full_ref,
    vec_ref,
    vdp_ref,
    vec2_ref,
    vz_ref,
    vec3_ref,
    vy_ref,
    p_send,
    p_recv,
    m_send,
    m_recv,
    s_send,
    s_recv,
    d_send,
    d_recv,
    rs_send,
    rs_recv,
    ag_send,
    ag_recv,
    v_send,
    v_recv,
    t_send,
    t_recv,
    in_sems,
):
    core = lax.axis_index("dp")
    k = lax.axis_index("seq")
    head = lax.axis_index("head")
    y = over(k, RING)
    z = left_over(k, RING)
    right = lax.rem(k + 1, SEQ)
    left = lax.rem(k + SEQ - 1, SEQ)
    up = lax.rem(k + RING, SEQ)
    down = lax.rem(k + SEQ - RING, SEQ)

    peers = [{"dp": 1 - core}]
    peers += [{"seq": y * RING + lax.rem(z + d, RING)} for d in range(1, RING)]
    peers += [{"seq": lax.rem(y + d, ROWS) * RING + z} for d in range(1, ROWS)]
    peers += [{"head": lax.rem(head + d, HEADS_AX)} for d in range(1, HEADS_AX)]
    load_x = pltpu.make_async_copy(x_hbm, x_ref, in_sems.at[0])
    load_dy = pltpu.make_async_copy(dy_hbm, dy_ref, in_sems.at[1])
    load_x.start()
    load_dy.start()
    barrier = pltpu.get_barrier_semaphore()
    for peer in peers:
        pl.semaphore_signal(barrier, inc=1, device_id=peer, device_id_type=MESH)

    lens = len_ref[...].astype(F32)
    docs = lens.shape[1]
    sub, lane = iota((docs, docs), 0), iota((docs, docs), 1)
    lens_col = jnp.sum(jnp.where(sub == lane, lens, 0.0), axis=1, keepdims=True)
    ends_row = jnp.sum(jnp.where(sub <= lane, lens_col, 0.0), axis=0, keepdims=True)
    ends_col = jnp.sum(jnp.where(lane <= sub, lens, 0.0), axis=1, keepdims=True)
    anchor = k * TOK
    pos_c = (anchor + iota((TOK, docs), 0)).astype(F32)
    pos_r = (anchor + iota((docs, TOK), 1)).astype(F32)
    one_r = (anchor + iota((1, docs), 0)).astype(F32)
    doc_c = jnp.sum(jnp.where(ends_row <= pos_c, 1.0, 0.0), axis=1, keepdims=True)
    doc_r = jnp.sum(jnp.where(ends_col <= pos_r, 1.0, 0.0), axis=0, keepdims=True)
    before = jnp.sum(jnp.where(ends_row <= one_r - 1.0, 1.0, 0.0), axis=1, keepdims=True)
    before = jnp.where(one_r[:, :1] < 0.5, -1.0, before)
    last = jnp.sum(jnp.where(ends_row <= one_r + (TOK - 1.0), 1.0, 0.0), axis=1, keepdims=True)
    enter = jnp.where(doc_c == before, 1.0, 0.0)
    leave = jnp.where(doc_c == last, 1.0, 0.0)
    same_end = jnp.where(last == before, 1.0, 0.0)

    bq, cq = b_ref[...], c_ref[...]
    rows, cols = iota((TOK, TOK), 0), iota((TOK, TOK), 1)
    cm, bm = cq.astype(F32) * enter, bq.astype(F32) * leave
    cb_ref[0], cb_ref[1] = cm.astype(BF16), bm.astype(BF16)
    cbt_ref[0], cbt_ref[1] = cm.T.astype(BF16), bm.T.astype(BF16)

    hsub, hlane = iota((HEADS, HEADS), 0), iota((HEADS, HEADS), 1)
    rate_col = jnp.sum(jnp.where(hsub == hlane, rate_ref[...], 0.0), axis=1, keepdims=True)
    skip_col = jnp.sum(jnp.where(hsub == hlane, skip_ref[...], 0.0), axis=1, keepdims=True)
    step = step_ref[...]
    tri = jnp.where(rows >= cols, 1.0, 0.0).astype(BF16)
    owner = jnp.where(over(iota((HEADS, FEAT), 1), HEAD_DIM) == iota((HEADS, FEAT), 0), 1.0, 0.0)
    ob_ref[...] = owner.astype(BF16)
    skx_ref[...] = jnp.sum(owner * skip_col, axis=0, keepdims=True)
    running = sum(nt(tri, part) for part in split3(-(step * rate_col)))
    rt_ref[0], rt_ref[1], rt_ref[2] = split3(running)

    def remote(src, dst, send, recv, device):
        return pltpu.make_async_remote_copy(
            src_ref=src,
            dst_ref=dst,
            send_sem=send,
            recv_sem=recv,
            device_id=device,
            device_id_type=MESH,
        )

    passing = jnp.exp(running[TOK - 1 :, :]) * same_end
    wide = jnp.concatenate([passing, jnp.zeros((1, 128 - HEADS), F32)], axis=1)
    thz_ref[z] = jnp.broadcast_to(wide, (8, 128))

    def copy_t(d, slot):
        target = y * RING + lax.rem(z + d, RING)
        return remote(
            thz_ref.at[z], thz_ref.at[slot], t_send.at[d], t_recv.at[d], {"seq": target}
        )

    def prepare(i):
        at = pl.ds(pl.multiple_of(i * WIDE, WIDE), WIDE)
        ob = ob_ref[:, at]
        rx = nn(rt_ref[0], ob) + nn(rt_ref[1], ob) + nn(rt_ref[2], ob)
        end = rx[TOK - 1 : TOK, :]
        mid = 0.5 * end
        em = jnp.exp(mid - rx)
        em_ref[:, at] = em
        x_f, dy_f = x_ref[:, at].astype(F32), dy_ref[:, at].astype(F32)
        sk_ref[:, at] = jnp.broadcast_to(jnp.sum(x_f * dy_f, axis=0, keepdims=True), (8, WIDE))
        xh, xl = split2(em * x_f)
        dyh, dyl = split2(jnp.exp(rx - mid) * dy_f)
        xh_ref[:, at], xl_ref[:, at], dyh_ref[:, at], dyl_ref[:, at] = xh, xl, dyh, dyl
        g = jnp.exp(mid)
        th = jnp.exp(end) * same_end
        local = g * (nn(cbt_ref[1], xh) + nn(cbt_ref[1], xl))
        local_d = g * (nn(cbt_ref[0], dyh) + nn(cbt_ref[0], dyl))
        for q in range(2):
            cut = slice(q * 128, q * 128 + 128)
            g_ref[2 * i + q] = jnp.broadcast_to(g[:, cut], (8, 128))
            th_ref[2 * i + q] = jnp.broadcast_to(th[:, cut], (8, 128))
            for n in range(PIECES):
                some = slice(n * HALF, n * HALF + HALF)
                l_ref[PER * i + PIECES * q + n] = local[some, cut]
                ld_ref[PER * i + PIECES * q + n] = local_d[some, cut]

    def choose(place):
        chosen = 0
        for n in range(1, GROUPS):
            chosen = jnp.where(place == n, ORDER[n], chosen)
        return chosen

    def prepare_next(place, _):
        prepare(choose(place))
        return 0

    load_x.wait()
    load_dy.wait()
    lax.fori_loop(0, READY, prepare_next, 0)
    pl.semaphore_wait(barrier, len(peers))
    for d in range(1, RING):
        copy_t(d, z).start()

    def make_weights():
        for d in range(1, RING):
            copy_t(d, lax.rem(z + RING - d, RING)).wait()
        ones = jnp.ones((8, 128), F32)
        ahead, behind = ones, ones
        for n in range(RING):
            ahead = ahead * jnp.where(n < z, thz_ref[n], ones)
            behind = behind * jnp.where(n > z, thz_ref[n], ones)
        pick = iota((8, 128), 0)
        row = ahead * behind * thz_ref[z]
        table = jnp.where(pick == 0, ahead, jnp.where(pick == 1, behind, row))
        table = sum(nn(part[:, :HEADS], ob_ref[...]) for part in split3(table))
        for n in range(FEAT // 128):
            w_ref[n] = table[:, n * 128 : (n + 1) * 128]

    def make_scores():
        same = doc_c == doc_r
        lower = same & (iota((TOK, TOK), 0) >= iota((TOK, TOK), 1))
        upper = same & (iota((TOK, TOK), 0) <= iota((TOK, TOK), 1))
        sm_ref[0], sm_ref[1] = split2(jnp.where(lower, nt(c_ref[...], b_ref[...]), 0.0))
        smt_ref[0], smt_ref[1] = split2(jnp.where(upper, nt(b_ref[...], c_ref[...]), 0.0))
        mask_ref[...] = jnp.where(lower, 1.0, 0.0)

    w_ref[...] = jnp.ones_like(w_ref)
    acc_ref[...] = jnp.zeros_like(acc_ref)
    rc_ref[...] = jnp.zeros_like(rc_ref)
    ds_ref[...] = jnp.zeros_like(ds_ref)

    def copy_p(part, s):
        return remote(
            send_p.at[part, s],
            recv_p.at[part, s],
            p_send.at[part, s],
            p_recv.at[part, s],
            {"seq": right},
        )

    def copy_m(part, s):
        return remote(
            send_m.at[part, s],
            recv_m.at[part, s],
            m_send.at[part, s],
            m_recv.at[part, s],
            {"seq": left},
        )

    def copy_s(s):
        return remote(ysend_s.at[s], cin_s.at[s], s_send.at[s], s_recv.at[s], {"seq": up})

    def copy_d(s):
        return remote(ysend_d.at[s], cin_d.at[s], d_send.at[s], d_recv.at[s], {"seq": down})

    def weights(s):
        fb = over(s, PIECES)
        return th_ref[fb, 0:1], w_ref[fb, 0:1], w_ref[fb, 1:2], w_ref[fb, 2:3]

    def chain(part, s, first, final, copy, recv, send, make):
        @pl.when(first)
        def _():
            recv[part, s] = jnp.zeros((HALF, 128), F32)

        @pl.when(jnp.logical_not(first))
        def _():
            copy(part, s).wait_recv()

        for late in range(2):

            @pl.when(s >= LATE if late else s < LATE)
            def _():
                send[part, s] = make(late, recv[part, s])

        @pl.when(jnp.logical_not(final))
        def _():
            copy(part, s).start()

    def pass_on(s, has_recv, has_send, copy, cin, ysend, total):
        @pl.when(has_recv)
        def _():
            copy(s).wait_recv()

        @pl.when(jnp.logical_not(has_recv))
        def _():
            cin[s] = jnp.zeros((HALF, 128), F32)

        @pl.when(has_send)
        def _():
            ysend[s] = total(s) + weights(s)[3] * cin[s]
            copy(s).start()

    def pass_s(s, total):
        pass_on(s, y > 0, y < ROWS - 1, copy_s, cin_s, ysend_s, total)

    def pass_d(s, total):
        pass_on(s, y < ROWS - 1, y > 0, copy_d, cin_d, ysend_d, total)

    def keep(s, state, cin, dest):
        cin[s] = state
        dest[0, s], dest[1, s] = split2(state * g_ref[over(s, PIECES), 0:1])

    def own_heads(i):
        shape = (WIDE, 128)
        hit = over(iota(shape, 0), HEAD_DIM) + 4 * i == iota(shape, 1)
        return jnp.where(hit, 1.0, 0.0).astype(BF16)

    def add_products(i, at, y_part, dx_part, extra):
        dyp = dyh_ref[:, at].astype(F32) + dyl_ref[:, at].astype(F32)
        xp = xh_ref[:, at].astype(F32) + xl_ref[:, at].astype(F32)
        prod = dyp * y_part - xp * dx_part
        if extra is not None:
            prod = prod + jnp.where(iota((TOK, WIDE), 0) == TOK - 1, extra, 0.0)
        heads = own_heads(i)
        rc_ref[...] += sum(nn(part, heads) for part in split3(prod))

    def local_work(i, turn):
        at = pl.ds(pl.multiple_of(i * WIDE, WIDE), WIDE)

        @pl.when(turn == 0)
        def _():
            yl_ref[...] = (
                nn(sm_ref[0], xh_ref[:, at])
                + nn(sm_ref[0], xl_ref[:, at])
                + nn(sm_ref[1], xh_ref[:, at])
            )

        @pl.when(turn == 1)
        def _():
            dx_ref[:, at] = (
                nn(smt_ref[0], dyh_ref[:, at])
                + nn(smt_ref[0], dyl_ref[:, at])
                + nn(smt_ref[1], dyh_ref[:, at])
            )

        @pl.when(turn == 2)
        def _():
            add_products(i, at, yl_ref[...], dx_ref[:, at], None)

        @pl.when(turn == 3)
        def _():
            ds_ref[...] += (
                nt(dyh_ref[:, at], xh_ref[:, at])
                + nt(dyh_ref[:, at], xl_ref[:, at])
                + nt(dyl_ref[:, at], xh_ref[:, at])
            )

    def states(ref, part, i):
        def column(q):
            some = [ref[part, PER * i + PIECES * q + n] for n in range(PIECES)]
            return jnp.concatenate(some, axis=0)

        return jnp.concatenate([column(0), column(1)], axis=1)

    def grads(i):
        at = pl.ds(pl.multiple_of(i * WIDE, WIDE), WIDE)
        sh, sl = states(sp_ref, 0, i), states(sp_ref, 1, i)
        dh, dl = states(dp_ref, 0, i), states(dp_ref, 1, i)
        xh, xl, dyh, dyl = xh_ref[:, at], xl_ref[:, at], dyh_ref[:, at], dyl_ref[:, at]
        acc_ref[:, :STATE] += nt(xh, dh) + nt(xl, dh) + nt(xh, dl)
        acc_ref[:, STATE:] += nt(dyh, sh) + nt(dyl, sh) + nt(dyh, sl)
        y_part = nn(cb_ref[0], sh) + nn(cb_ref[0], sl)
        dx_part = nn(cb_ref[1], dh) + nn(cb_ref[1], dl)
        ends = []
        for q in range(2):
            total = 0.0
            for n in range(PIECES):
                s = PER * i + PIECES * q + n
                out = th_ref[2 * i + q, 0:1] * cin_s[s] + l_ref[s]
                total = total + jnp.sum(out * cin_d[s], axis=0, keepdims=True)
            ends.append(total)
        add_products(i, at, y_part, dx_part, jnp.concatenate(ends, axis=1))
        whole = em_ref[:, at] * (dx_ref[:, at] + dx_part)
        whole = whole + skx_ref[:, at] * dy_ref[:, at].astype(F32)
        gx_ref[:, at] = whole.astype(BF16)

    from_left = over(HOP * z, 4)
    from_right = over(HOP * (RING - 1 - z), 4)
    far = jnp.maximum(from_left, from_right)
    need = jnp.where((z == 0) | (z == RING - 1), DELAY, over(HOP, 4))
    hops_s, hops_d = y, ROWS - 1 - y

    def slot_body(tau, _):
        def at(n, low, high, work):
            @pl.when((n >= low) & (n < high))
            def _():
                work(n)

        def run(forward, part, s):
            th, ahead, behind, _ = weights(s)
            weight = ahead if forward else behind
            mine, other = (l_ref, ld_ref) if forward else (ld_ref, l_ref)
            cin_mine, cin_other = (cin_s, cin_d) if forward else (cin_d, cin_s)

            def make(late, value):
                if part:
                    return value + (cin_other[s] if late else weight * other[s])
                if late:
                    value = value + weight * cin_mine[s]
                return th * value + mine[s]

            ends = (z == 0, z == RING - 1) if forward else (z == RING - 1, z == 0)
            copy, recv, send = (copy_p, recv_p, send_p) if forward else (copy_m, recv_m, send_m)
            chain(part, s, *ends, copy, recv, send, make)

        at(tau - from_left, 0, SLICES, lambda s: run(True, 0, s))
        at(tau - from_right, 0, SLICES, lambda s: run(False, 0, s))

        @pl.when(tau == need)
        def _():
            make_weights()

        at(tau - from_left, 0, SLICES, lambda s: run(True, 1, s))
        at(tau - from_right, 0, SLICES, lambda s: run(False, 1, s))

        def early_s(s):
            pass_s(s, lambda s: weights(s)[2] * l_ref[s])

        def early_d(s):
            pass_d(s, lambda s: weights(s)[1] * ld_ref[s])

        at(tau + LATE - DELAY - LAG * hops_s, LATE, SLICES, early_s)
        at(tau + LATE - DELAY - LAG * hops_d, LATE, SLICES, early_d)

        def late_s(s):
            pass_s(s, lambda s: weights(s)[2] * send_p[0, s] + recv_m[1, s])
            keep(s, recv_p[0, s] + weights(s)[1] * cin_s[s], cin_s, sp_ref)

        def late_d(s):
            pass_d(s, lambda s: weights(s)[1] * send_m[0, s] + recv_p[1, s])
            keep(s, recv_m[0, s] + weights(s)[2] * cin_d[s], cin_d, dp_ref)

        at(tau - far - LAG * hops_s, 0, LATE, late_s)
        at(tau - far - LAG * hops_d, 0, LATE, late_d)

        def whole(s):
            _, ahead, behind, _ = weights(s)
            state = recv_p[0, s] + ahead * (cin_s[s] + recv_m[1, s])
            state_d = recv_m[0, s] + behind * (cin_d[s] + recv_p[1, s])
            keep(s, state, cin_s, sp_ref)
            keep(s, state_d, cin_d, dp_ref)

        at(tau - far, LATE, SLICES, whole)

        @pl.when(tau == 1)
        def _():
            make_scores()

        beat = PER // 2
        place = over(tau, beat) + READY

        @pl.when((left_over(tau, beat) == 0) & (place < GROUPS))
        def _():
            prepare(choose(place))

        @pl.when(tau == SLICES + PER)
        def _():
            d_scores = jnp.where(mask_ref[...] > 0.5, ds_ref[...], 0.0)
            sh, sl = split2(d_scores)
            part_ref[1] = nn(sh, b_ref[...]) + nn(sl, b_ref[...])
            th, tl = split2(d_scores.T)
            part_ref[0] = nn(th, c_ref[...]) + nn(tl, c_ref[...])

        @pl.when(tau == SLICES + PER + 1)
        def _():
            skip_part = sum(nt(ob_ref[...], part) for part in split3(sk_ref[...]))[:, :1]
            diag = iota((HEADS, 128), 0) == iota((HEADS, 128), 1)
            skip_row = jnp.sum(jnp.where(diag, skip_part, 0.0), axis=0, keepdims=True)
            skr_ref[...] = jnp.broadcast_to(skip_row, (8, 128))

        turn = left_over(tau, PER)

        @pl.when((tau >= PER) & (tau < SLICES + PER) & (left_over(turn, PIECES // 2) == 0))
        def _():
            local_work(over(tau, PER) - 1, over(turn, PIECES // 2))

        def both(c, _):
            done = jnp.where(c == 0, tau - far - LAG * jnp.maximum(hops_s, hops_d), tau - far)
            done = done - (PER - 1)
            low = jnp.where(c == 0, 0, LATE)
            high = jnp.where(c == 0, LATE, SLICES)

            @pl.when((done >= low) & (done < high) & (left_over(done, PER) == 0))
            def _():
                grads(over(done, PER))

            return 0

        lax.fori_loop(0, 2, both, 0)
        return 0

    lax.fori_loop(0, SLOTS, slot_body, 0)

    quarter = TOK // HEADS_AX

    def copy_rs(n, d):
        target = lax.rem(head + d, HEADS_AX)
        rows_of = pl.ds(pl.multiple_of(target * quarter, quarter), quarter)
        return remote(
            part_ref.at[n, rows_of],
            rs_ref.at[n, d],
            rs_send.at[n, d],
            rs_recv.at[n, d],
            {"head": target},
        )

    def copy_ag(n, d, slot):
        return remote(
            sum_ref.at[n],
            full_ref.at[n, slot],
            ag_send.at[n, d],
            ag_recv.at[n, d],
            {"head": lax.rem(head + d, HEADS_AX)},
        )

    part_ref[1] += enter * acc_ref[:, STATE:]
    for d in range(1, HEADS_AX):
        copy_rs(1, d).start()
    part_ref[0] += leave * acc_ref[:, :STATE]
    for d in range(1, HEADS_AX):
        copy_rs(0, d).start()

    tri = jnp.where(iota((TOK, TOK), 0) >= iota((TOK, TOK), 1), 1.0, 0.0).astype(BF16)
    dl = sum(nn(part[:HEADS], tri) for part in split3(rc_ref[...].T))
    gs_ref[...] = -(rate_col * dl)
    rate_part = -jnp.sum(step * dl, axis=1, keepdims=True)
    diag = iota((HEADS, 128), 0) == iota((HEADS, 128), 1)
    rate_row = jnp.sum(jnp.where(diag, rate_part, 0.0), axis=0, keepdims=True)
    first = iota((8, 128), 0)
    vec_ref[...] = jnp.where(first == 0, rate_row, jnp.where(first == 1, skr_ref[...], 0.0))

    swap = remote(vec_ref, vdp_ref, v_send.at[0], v_recv.at[0], {"dp": 1 - core})
    swap.start()
    swap.wait()
    vec2_ref[...] = vec_ref[...] + vdp_ref[...]
    vz_ref[z] = vec2_ref[...]

    def copy_z(d, slot):
        target = y * RING + lax.rem(z + d, RING)
        return remote(vec2_ref, vz_ref.at[slot], v_send.at[d], v_recv.at[d], {"seq": target})

    for d in range(1, RING):
        copy_z(d, z).start()
    mine_rows = pl.ds(pl.multiple_of(head * quarter, quarter), quarter)
    def drain(s, _):
        @pl.when(z < RING - 1)
        def _():
            copy_p(0, s).wait_send()
            copy_p(1, s).wait_send()

        @pl.when(z > 0)
        def _():
            copy_m(0, s).wait_send()
            copy_m(1, s).wait_send()

        @pl.when(y < ROWS - 1)
        def _():
            copy_s(s).wait_send()

        @pl.when(y > 0)
        def _():
            copy_d(s).wait_send()

        return 0

    lax.fori_loop(0, SLICES, drain, 0)

    for n in (1, 0):
        for d in range(1, HEADS_AX):
            copy_rs(n, d).wait()
        sum_ref[n] = part_ref[n, mine_rows] + rs_ref[n, 1] + rs_ref[n, 2] + rs_ref[n, 3]
        full_ref[n, head] = sum_ref[n]
        for d in range(1, HEADS_AX):
            copy_ag(n, d, head).start()

    for d in range(1, RING):
        copy_z(d, lax.rem(z + RING - d, RING)).wait()
    vec3_ref[...] = sum(vz_ref[n] for n in range(RING))
    vy_ref[y] = vec3_ref[...]

    def copy_y(d, slot):
        target = lax.rem(y + d, ROWS) * RING + z
        n = RING + d
        return remote(vec3_ref, vy_ref.at[slot], v_send.at[n], v_recv.at[n], {"seq": target})

    for d in range(1, ROWS):
        copy_y(d, y).start()
    for n, out_ref in ((1, gc_ref), (0, gb_ref)):
        for d in range(1, HEADS_AX):
            copy_ag(n, d, lax.rem(head + HEADS_AX - d, HEADS_AX)).wait()
        for m in range(HEADS_AX):
            out_ref[m * quarter : (m + 1) * quarter] = full_ref[n, m]
    for d in range(1, ROWS):
        copy_y(d, lax.rem(y + ROWS - d, ROWS)).wait()
    whole_vec = sum(vy_ref[n] for n in range(ROWS))
    gr_ref[...] = whole_vec[0:1, :HEADS]
    gk_ref[...] = whole_vec[1:2, :HEADS]


def hand_out(*refs):
    ins, outs, held, sems_in, sems_out = refs[:6], refs[6:12], refs[12:18], refs[18], refs[19]
    pieces = [(n, None) for n in range(1, 6)]
    pieces = [(0, pl.ds(m * TOK // 4, TOK // 4)) for m in range(4)] + pieces

    def cut(ref, rows):
        return ref if rows is None else ref.at[rows]

    loads, stores = [], []
    for m, (n, rows) in enumerate(pieces):
        there, here, out = cut(ins[n], rows), cut(held[n], rows), cut(outs[n], rows)
        loads.append(pltpu.make_async_copy(there, here, sems_in.at[m]))
        stores.append(pltpu.make_async_copy(here, out, sems_out.at[m]))
    for load in loads:
        load.start()
    for load, store in zip(loads, stores):
        load.wait()
        store.start()
    for store in stores:
        store.wait()


def on_device(inputs, proj_b, proj_c, step_size, decay_rate, skip_gain, doc_lengths, grad_out):
    vmem = pl.BlockSpec(memory_space=pltpu.VMEM)
    state = pltpu.VMEM((SLICES, HALF, 128), F32)
    message = pltpu.VMEM((2, SLICES, HALF, 128), F32)
    pair = pltpu.VMEM((2, SLICES, HALF, 128), BF16)
    sems = pltpu.SemaphoreType.DMA((SLICES,))
    both = pltpu.SemaphoreType.DMA((2, SLICES))
    tile = pltpu.VMEM((8, 128), F32)
    quarter = TOK // HEADS_AX
    scratch = [
        pltpu.VMEM((TOK, FEAT), BF16),
        pltpu.VMEM((TOK, FEAT), BF16),
        pltpu.VMEM((TOK, FEAT), BF16),
        pltpu.VMEM((TOK, FEAT), BF16),
        pltpu.VMEM((TOK, FEAT), BF16),
        pltpu.VMEM((TOK, FEAT), BF16),
        pltpu.VMEM((TOK, FEAT), F32),
        pltpu.VMEM((TOK, FEAT), F32),
        pltpu.VMEM((TOK, WIDE), F32),
        pltpu.VMEM((HEADS, FEAT), BF16),
        pltpu.VMEM((3, TOK, HEADS), BF16),
        pltpu.VMEM((2, TOK, TOK), BF16),
        pltpu.VMEM((2, TOK, TOK), BF16),
        pltpu.VMEM((TOK, TOK), F32),
        pltpu.VMEM((2, TOK, STATE), BF16),
        pltpu.VMEM((2, STATE, TOK), BF16),
        pltpu.VMEM((FEAT // 128, 8, 128), F32),
        pltpu.VMEM((FEAT // 128, 8, 128), F32),
        pltpu.VMEM((FEAT // 128, 8, 128), F32),
        pltpu.VMEM((RING, 8, 128), F32),
        pltpu.VMEM((TOK, TOK), F32),
        tile,
        pltpu.VMEM((1, FEAT), F32),
        pltpu.VMEM((8, FEAT), F32),
        pltpu.VMEM((TOK, 128), F32),
        state,
        state,
        message,
        message,
        message,
        message,
        state,
        state,
        state,
        state,
        pair,
        pair,
        pltpu.VMEM((TOK, 2 * STATE), F32),
        pltpu.VMEM((2, TOK, STATE), F32),
        pltpu.VMEM((2, HEADS_AX, quarter, STATE), F32),
        pltpu.VMEM((2, quarter, STATE), F32),
        pltpu.VMEM((2, HEADS_AX, quarter, STATE), F32),
        tile,
        tile,
        tile,
        pltpu.VMEM((RING, 8, 128), F32),
        tile,
        pltpu.VMEM((ROWS, 8, 128), F32),
        both,
        both,
        both,
        both,
        sems,
        sems,
        sems,
        sems,
        pltpu.SemaphoreType.DMA((2, HEADS_AX)),
        pltpu.SemaphoreType.DMA((2, HEADS_AX)),
        pltpu.SemaphoreType.DMA((2, HEADS_AX)),
        pltpu.SemaphoreType.DMA((2, HEADS_AX)),
        pltpu.SemaphoreType.DMA((RING + ROWS,)),
        pltpu.SemaphoreType.DMA((RING + ROWS,)),
        pltpu.SemaphoreType.DMA((RING,)),
        pltpu.SemaphoreType.DMA((RING,)),
        pltpu.SemaphoreType.DMA((2,)),
    ]
    shapes = (
        jax.ShapeDtypeStruct((TOK, FEAT), BF16),
        jax.ShapeDtypeStruct((TOK, STATE), F32),
        jax.ShapeDtypeStruct((TOK, STATE), F32),
        jax.ShapeDtypeStruct((HEADS, TOK), F32),
        jax.ShapeDtypeStruct((1, HEADS), F32),
        jax.ShapeDtypeStruct((1, HEADS), F32),
    )
    anywhere = pl.BlockSpec(memory_space=pl.ANY)
    results = pl.pallas_call(
        kernel,
        out_shape=shapes,
        in_specs=[anywhere] * 2 + [vmem] * 6,
        out_specs=(vmem,) * 6,
        scratch_shapes=scratch,
        compiler_params=pltpu.CompilerParams(
            collective_id=0, has_side_effects=True, vmem_limit_bytes=56 << 20
        ),
    )(
        inputs[0],
        grad_out[0],
        proj_b[0],
        proj_c[0],
        step_size[0],
        decay_rate[None],
        skip_gain[None],
        doc_lengths,
    )
    grad_x, grad_b, grad_c, grad_step, grad_rate, grad_skip = pl.pallas_call(
        hand_out,
        out_shape=shapes,
        in_specs=[anywhere] * 6,
        out_specs=(anywhere,) * 6,
        scratch_shapes=[pltpu.VMEM(shape.shape, shape.dtype) for shape in shapes]
        + [pltpu.SemaphoreType.DMA((9,)), pltpu.SemaphoreType.DMA((9,))],
        compiler_params=pltpu.CompilerParams(vmem_limit_bytes=56 << 20),
    )(*results)
    return (
        grad_x[None],
        grad_b[None],
        grad_c[None],
        grad_step[None],
        grad_rate[0],
        grad_skip[0],
    )


def solution(mesh):
    in_specs = (
        P("dp", "seq", "head"),
        P("dp", "seq", None),
        P("dp", "seq", None),
        P("dp", "head", "seq"),
        P("head"),
        P("head"),
        P("dp", None),
        P("dp", "seq", "head"),
    )
    out_specs = (
        P("dp", "seq", "head"),
        P("dp", "seq", None),
        P("dp", "seq", None),
        P("dp", "head", "seq"),
        P("head"),
        P("head"),
    )
    return jax.shard_map(
        on_device, mesh=mesh, in_specs=in_specs, out_specs=out_specs, check_vma=False
    )
```
